32 devices in a mesh: row: 4 (over z), col: 8 (over y, x, core).
Axes of the slice: x: 2, y: 2, z: 4, core: 2. Of those that a mesh axis runs over, the one named last changes fastest.
Arguments:
- h_values: float32 [4, 64, 4096], P('row', 'col'), as said below
- h_places: int32 [4, 64], P('row', 'col'), may hold values from 0 to 7, as said below
- h_counts: int32 [4, 8], P('row', 'col'), may hold values from 0 to 8, as said below
- p_values: float32 [4, 64, 4096], P('row', 'col'), as said below
- p_places: int32 [4, 64], P('row', 'col'), may hold values from 0 to 7, as said below
- p_counts: int32 [4, 8], P('row', 'col'), may hold values from 0 to 8, as said below
- s_values: float32 [4, 64, 4096], P('row', 'col'), as said below
- s_places: int32 [4, 64], P('row', 'col'), may hold values from 0 to 7, as said below
- s_counts: int32 [4, 8], P('row', 'col'), may hold values from 0 to 8, as said below
- x_places: int32 [4, 64], P('row', 'col'), may hold values from 0 to 7, as said below
- x_counts: int32 [4, 8], P('row', 'col'), may hold values from 0 to 8, as said below
Outputs:
- gradient: float32 [4, 64, 4096], P('row', 'col')
The draws below stay inside these ranges and needn't reach their ends.
Inputs may be any that keep to these rules, and one draw needn't show every extreme that they name: `h_places`: in each tile the 8 entries are a permutation of the tile's positions; the first count entries are the present blocks. Every pattern is symmetric, holds every block whose block row and block column lie in the same row panel, and every block (i, j) whose cyclic block distance min(|i - j|, 16 - |i - j|) is 2 or less or exactly 8. `p_places`: as for h_places. `s_places`: as for h_places. `x_places`: as for h_places. `h_counts`: every tile whose block columns lie in its own row panel is full. `p_counts`: as for h_counts. `s_counts`: as for h_counts. `x_counts`: as for h_counts. `h_values`: the assembled H is symmetric. `p_values`: the assembled P is symmetric. `s_values`: the assembled S is symmetric.
All inputs are finite; a program needn't handle non-finite values.
Results may differ from the reference program's by a relative error of at most 0.000088.
Values sent between devices are 32-bit elements; how exact they have to be, the bound alone decides.
No kernel may reach another device: no remote copies, remote signals or barrier semaphores. Data moves between devices by JAX's collectives and lax.ppermute only.
A program may use at most 64 MiB of HBM per device.

```python
import jax
import jax.numpy as jnp
from jax import lax

BS = 64
TC = 2
NB = 16
TR = 4
CAP = 8
ORDER = 1024


def pattern(key, salt_value):
    base = jax.random.fold_in(key, salt_value)
    first_key, second_key, third_key = jax.random.split(base, 3)
    panel_rows = NB // TR
    panel_cols = NB // TC
    random_codes = jax.random.randint(first_key, (NB, NB), 0, 4)
    symmetric = jnp.minimum(random_codes, random_codes.T)
    block_ids = jnp.arange(NB)
    distance_raw = jnp.abs(block_ids[:, None] - block_ids[None, :])
    distance = jnp.minimum(distance_raw, NB - distance_raw)
    offsets = jax.random.randint(third_key, (3,), 3, NB // 2 + 1)
    on_far = jnp.any(distance[..., None] == offsets[None, None, :], axis=-1) & (symmetric > 0)
    half_box = distance == NB // 2
    same_panel = block_ids[:, None] // TR == block_ids[None, :] // TR
    present = (same_panel | (distance <= 2) | on_far | half_box).astype(jnp.int32)
    tile_flags = present.reshape(panel_rows, TR, panel_cols, TC).transpose(0, 2, 1, 3).reshape(panel_rows, panel_cols, CAP)
    shuffle = jax.random.randint(second_key, (panel_rows, panel_cols, CAP), 0, 2 ** 20)
    ranking_keys = (1 - tile_flags) * 2 ** 25 + shuffle * CAP + jnp.arange(CAP)
    places = jnp.argsort(ranking_keys, axis=-1, stable=True).astype(jnp.int32)
    counts = jnp.sum(tile_flags, axis=-1).astype(jnp.int32)
    return (places, counts)


def matrix_values(key, salt_value):
    places, counts = pattern(key, salt_value)
    panel_rows = NB // TR
    panel_cols = NB // TC
    value_key = jax.random.fold_in(key, salt_value + 100)
    raw_entries = jax.random.normal(value_key, (ORDER, ORDER), jnp.float32)
    factor = (0.5 / (BS * (TR + 5))) ** (1.0 / 3.0)
    full_matrix = (raw_entries + raw_entries.T) * factor
    blocks = full_matrix.reshape(panel_rows, TR, BS, panel_cols, TC, BS).transpose(0, 3, 1, 4, 2, 5)
    blocks = blocks.reshape(panel_rows, panel_cols, CAP, BS * BS)
    picked = jnp.take_along_axis(blocks, places[..., None], axis=2)
    return picked.reshape(panel_rows, panel_cols * CAP, BS * BS)


def list_of(key, salt_value):
    places, counts = pattern(key, salt_value)
    return places.reshape(NB // TR, NB // TC * CAP)


def count_of(key, salt_value):
    places, counts = pattern(key, salt_value)
    return counts


def draw_h_values(key, part):
    return matrix_values(key, 11)


def draw_h_places(key, part):
    return list_of(key, 11)


def draw_h_counts(key, part):
    return count_of(key, 11)


def draw_p_values(key, part):
    return matrix_values(key, 23)


def draw_p_places(key, part):
    return list_of(key, 23)


def draw_p_counts(key, part):
    return count_of(key, 23)


def draw_s_values(key, part):
    return matrix_values(key, 37)


def draw_s_places(key, part):
    return list_of(key, 37)


def draw_s_counts(key, part):
    return count_of(key, 37)


def draw_x_places(key, part):
    return list_of(key, 41)


def draw_x_counts(key, part):
    return count_of(key, 41)


def setup_inputs(seed: int = 0) -> dict:
    streams_of = jax.random.split(jax.random.key(seed), 12)
    h_values = draw_h_values(jax.random.fold_in(streams_of[11], 71), 0)
    h_places = draw_h_places(jax.random.fold_in(streams_of[11], 71), 0)
    h_counts = draw_h_counts(jax.random.fold_in(streams_of[11], 71), 0)
    p_values = draw_p_values(jax.random.fold_in(streams_of[11], 71), 0)
    p_places = draw_p_places(jax.random.fold_in(streams_of[11], 71), 0)
    p_counts = draw_p_counts(jax.random.fold_in(streams_of[11], 71), 0)
    s_values = draw_s_values(jax.random.fold_in(streams_of[11], 71), 0)
    s_places = draw_s_places(jax.random.fold_in(streams_of[11], 71), 0)
    s_counts = draw_s_counts(jax.random.fold_in(streams_of[11], 71), 0)
    x_places = draw_x_places(jax.random.fold_in(streams_of[11], 71), 0)
    x_counts = draw_x_counts(jax.random.fold_in(streams_of[11], 71), 0)
    return dict(h_values=h_values, h_places=h_places, h_counts=h_counts, p_values=p_values, p_places=p_places, p_counts=p_counts, s_values=s_values, s_places=s_places, s_counts=s_counts, x_places=x_places, x_counts=x_counts)


def assemble(values, places, counts):
    panel_rows = NB // TR
    panel_cols = NB // TC
    blocks_in = values.reshape(panel_rows, panel_cols, CAP, BS * BS).astype(jnp.float32)
    positions = places.reshape(panel_rows, panel_cols, CAP)
    slot_ids = jnp.arange(CAP, dtype=jnp.int32)
    matches = (positions[..., None] == slot_ids) & (slot_ids[:, None] < counts[..., None, None])
    tiles = jnp.einsum("rcsp,rcsv->rcpv", matches.astype(jnp.float32), blocks_in, precision=lax.Precision.HIGHEST)
    tiles = tiles.reshape(panel_rows, panel_cols, TR, TC, BS, BS)
    return tiles.transpose(0, 2, 4, 1, 3, 5).reshape(ORDER, ORDER)


def pattern_mask(places, counts):
    panel_rows = NB // TR
    panel_cols = NB // TC
    positions = places.reshape(panel_rows, panel_cols, CAP)
    slot_ids = jnp.arange(CAP, dtype=jnp.int32)
    matches = (positions[..., None] == slot_ids) & (slot_ids[:, None] < counts[..., None, None])
    present = jnp.sum(matches.astype(jnp.float32), axis=2)
    present = present.reshape(panel_rows, panel_cols, TR, TC).transpose(0, 2, 1, 3).reshape(NB, NB)
    return jnp.broadcast_to(present[:, None, :, None], (NB, BS, NB, BS)).reshape(ORDER, ORDER)


def to_slots(matrix, places, counts):
    panel_rows = NB // TR
    panel_cols = NB // TC
    blocks = matrix.reshape(panel_rows, TR, BS, panel_cols, TC, BS).transpose(0, 3, 1, 4, 2, 5)
    blocks = blocks.reshape(panel_rows, panel_cols, CAP, BS * BS)
    positions = places.reshape(panel_rows, panel_cols, CAP).astype(jnp.int32)
    picked = jnp.take_along_axis(blocks, positions[..., None], axis=2)
    slot_ids = jnp.arange(CAP, dtype=jnp.int32)
    used = (slot_ids[None, None, :] < counts[..., None]).astype(matrix.dtype)
    picked = picked * used[..., None]
    return picked.reshape(panel_rows, panel_cols * CAP, BS * BS)


def reference(h_values, h_places, h_counts, p_values, p_places, p_counts, s_values, s_places, s_counts, x_places, x_counts):
    kohn_sham = assemble(h_values, h_places, h_counts)
    density = assemble(p_values, p_places, p_counts)
    intersection = assemble(s_values, s_places, s_counts)
    allowed = pattern_mask(x_places, x_counts)
    first = allowed * jnp.dot(kohn_sham, density, precision=lax.Precision.HIGHEST)
    second = allowed * jnp.dot(first, intersection, precision=lax.Precision.HIGHEST)
    return to_slots(second + second.T, x_places, x_counts)
```

```python
import functools

import jax
import jax.numpy as jnp
from jax import lax
from jax.experimental import pallas as pl
from jax.experimental.pallas import tpu as pltpu
from jax.sharding import PartitionSpec as P

BS = 64
LANES = 128
PAIR = 2 * LANES
LINES = BS * BS // LANES
VMEM = pl.BlockSpec(memory_space=pltpu.VMEM)
SMEM = pl.BlockSpec(memory_space=pltpu.SMEM)
AXES = ("row", "col")


def position():
    col = lax.axis_index("col")
    return lax.axis_index("row"), col // 2, col % 2


def left_lanes(rows):
    return lax.broadcasted_iota(jnp.int32, (rows, LANES), 1) < BS


def invert(places, inverse, base):
    cap = places.shape[1]
    for slot in range(cap):
        inverse[base + places[0, slot]] = slot


def assemble_kernel(*refs):
    values, places, counts = refs[0:3], refs[3:7], refs[7:11]
    out, lines, inverse = refs[11:]
    cap = values[0].shape[1]
    rows = cap * LINES
    left = left_lanes(LINES)
    for which in range(4):
        invert(places[which], inverse, which * cap)
    for which in range(3):
        for line in range(LINES):
            lines[which, pl.ds(line, cap, stride=LINES), :] = values[which][
                0, :, line * LANES : (line + 1) * LANES
            ]
        count = counts[which][0, 0]

        def block(place):
            slot = inverse[which * cap + place]
            kept = (slot < count).astype(jnp.float32)
            start = pl.multiple_of(slot * LINES, LINES)
            return lines[which, pl.ds(start, LINES), :] * kept

        for pair in range(cap // 2):
            first, second = block(2 * pair), block(2 * pair + 1)
            even = jnp.where(left, first, pltpu.roll(second, BS, 1))
            odd = jnp.where(left, pltpu.roll(first, BS, 1), second)
            start = which * rows + pair * BS
            out[pl.ds(start, LINES, stride=2), :] = even
            out[pl.ds(start + 1, LINES, stride=2), :] = odd
    count = counts[3][0, 0]
    for pair in range(cap // 2):
        flags = [
            (inverse[3 * cap + 2 * pair + side] < count).astype(jnp.float32) for side in range(2)
        ]
        out[3 * rows + pair : 3 * rows + pair + 1, :] = jnp.where(
            left_lanes(1), flags[0], flags[1]
        )


def pack_kernel(rows, combos, own, other, *outs):
    _, _, core = position()
    for k in range(2):

        @pl.when(core == k)
        def _():
            halves = (own, other) if k == 0 else (other, own)
            for combo, out in zip(combos, outs):
                start = "HPS".index(combo[k]) * rows
                for side in range(2):
                    out[:, side * LANES : (side + 1) * LANES] = halves[side][
                        start : start + rows, :
                    ]


def split(x):
    high = x.astype(jnp.bfloat16)
    return high, (x - high.astype(jnp.float32)).astype(jnp.bfloat16)


def dot3(a, b_high, b_low):
    a_high, a_low = split(a)
    dot = functools.partial(jnp.dot, preferred_element_type=jnp.float32)
    return dot(a_high, b_high) + (dot(a_high, b_low) + dot(a_low, b_high))


def store_split(high, low, start, rows, x, columns=slice(None)):
    h, l = split(x)
    high[pl.ds(start, rows), columns] = h
    low[pl.ds(start, rows), columns] = l


def masked(acc, halves, rows, k):
    count = acc.shape[0] // BS
    lines = []
    for line in range(count):
        at = 3 * rows + k * count + line
        row = jnp.concatenate([half[at : at + 1, :] for half in halves], axis=1)
        lines.append(acc[line * BS : (line + 1) * BS, :] * row)
    return jnp.concatenate(lines, axis=0)


def y_kernel(rows, ops, own, other, *refs):
    count = len(ops)
    got, shared = refs[:count], refs[count : 2 * count]
    out, high, low = refs[2 * count :]
    row, chip, core = position()
    half = rows // 2
    for k in range(2):

        @pl.when(core == k)
        def _():
            halves = (own, other) if k == 0 else (other, own)
            start = pl.multiple_of(row * rows, rows)
            for side in range(2):
                store_split(
                    high,
                    low,
                    start,
                    rows,
                    halves[side][rows : 2 * rows, :],
                    slice(side * LANES, (side + 1) * LANES),
                )
            pieces = []
            for i, op in enumerate(ops):
                for holder in range(2):
                    item = op[holder]
                    ref = got[i] if holder == k else shared[i]
                    if item is None or item[0] == "S":
                        continue
                    if item[0] == "P":
                        start = pl.multiple_of((row ^ item[1]) * rows, rows)
                        store_split(high, low, start, rows, ref[...])
                    else:
                        pieces.append((item[1], ref))
            mine = slice(k * half, (k + 1) * half)
            a = jnp.concatenate([ref[mine, :] for ref in halves], axis=1)
            at = pl.ds(pl.multiple_of(chip * PAIR, PAIR), PAIR)
            acc = dot3(a, high[at, :], low[at, :])
            for offset, ref in pieces:
                at = pl.ds(pl.multiple_of((chip ^ offset) * PAIR, PAIR), PAIR)
                acc += dot3(ref[mine, :], high[at, :], low[at, :])
            out[...] = masked(acc, halves, rows, k)


def x_kernel(rows, ops, offsets, parts, own, other, *refs):
    count = len(ops)
    got, shared = refs[:count], refs[count : 2 * count]
    y_refs = refs[2 * count : 2 * count + len(offsets)]
    out, swap = refs[2 * count + len(offsets) :][:2]
    sent = refs[2 * count + len(offsets) + 2 : -2]
    high, low = refs[-2:]
    row, chip, core = position()
    half = rows // 2
    for k in range(2):

        @pl.when(core == k)
        def _():
            halves = (own, other) if k == 0 else (other, own)
            start = pl.multiple_of(row * rows, rows)
            for side in range(2):
                store_split(
                    high,
                    low,
                    start,
                    rows,
                    halves[side][2 * rows : 3 * rows, :],
                    slice(side * LANES, (side + 1) * LANES),
                )
            for i, op in enumerate(ops):
                for holder in range(2):
                    item = op[holder]
                    ref = got[i] if holder == k else shared[i]
                    if item is not None and item[0] == "S":
                        start = pl.multiple_of((row ^ item[1]) * rows, rows)
                        store_split(high, low, start, rows, ref[...])
            acc = jnp.zeros((half, PAIR), jnp.float32)
            for offset, ref in zip(offsets, y_refs):
                at = pl.ds(pl.multiple_of((chip ^ offset) * PAIR, PAIR), PAIR)
                acc += dot3(ref[...], high[at, :], low[at, :])
            x = masked(acc, halves, rows, k)
            out[...] = x
            swap[...] = x[:, (1 - k) * LANES : (2 - k) * LANES]
    for turn, ref in enumerate(sent):
        part = (chip % parts + turn) % parts
        ref[...] = out[pl.ds(pl.multiple_of(part * LANES, LANES), LANES), :]


def slots_kernel(parts, places, counts, x, swapped, *refs):
    mirrors = refs[:parts]
    out, tile, lines, inverse = refs[parts:]
    _, _, core = position()
    cap = places.shape[1]
    half = x.shape[0]
    invert(places, inverse, 0)
    for k in range(2):

        @pl.when(core == k)
        def _():
            tile[k * half : (k + 1) * half, :] = x[:, k * LANES : (k + 1) * LANES]
            tile[(1 - k) * half : (2 - k) * half, :] = swapped[...]

    for turn in range(parts):
        col = lax.axis_index("col")
        at = ((col % parts) - turn + parts) % parts
        at = pl.ds(pl.multiple_of(at * PAIR, PAIR), PAIR)
        tile[at, :] += mirrors[turn][...].T
    count = counts[0, 0]
    left = left_lanes(LINES)
    for pair in range(cap // 2):
        even = tile[pl.ds(pair * BS, LINES, stride=2), :]
        odd = tile[pl.ds(pair * BS + 1, LINES, stride=2), :]
        blocks = (
            jnp.where(left, even, pltpu.roll(odd, BS, 1)),
            jnp.where(left, pltpu.roll(even, BS, 1), odd),
        )
        for side in range(2):
            slot = inverse[2 * pair + side]
            used = (slot < count).astype(jnp.float32)
            start = pl.multiple_of(slot * LINES, LINES)
            lines[pl.ds(start, LINES), :] = blocks[side] * used
    for line in range(LINES):
        out[0, :, line * LANES : (line + 1) * LANES] = lines[
            pl.ds(line, cap, stride=LINES), :
        ]


def call(kernel, out_shapes, in_specs, scratch, cost, *args):
    single = not isinstance(out_shapes, list)
    return pl.pallas_call(
        kernel,
        out_shape=out_shapes,
        in_specs=in_specs,
        out_specs=VMEM if single else [VMEM] * len(out_shapes),
        scratch_shapes=scratch,
        compiler_params=pltpu.CompilerParams(vmem_limit_bytes=32 * 1024 * 1024),
        cost_estimate=pl.CostEstimate(flops=cost, bytes_accessed=1 << 20, transcendentals=0),
    )(*args)


def queues(row_count, chip_count):
    along = sorted(range(1, row_count), key=lambda s: (s != 2, -s))
    across = list(range(chip_count - 1, 0, -1))
    first = [("H", o) for o in across]
    second = [("P", s) for s in along]
    for s in along:
        (first if len(first) < len(second) else second).append(("S", s))
    steps = max(len(first), len(second))
    first += [None] * (steps - len(first))
    second += [None] * (steps - len(second))
    return list(zip(first, second))


def shards(row_count, chip_count, hv, hp, hc, pv, pp, pc, sv, sp, sc, xp, xc):
    cap = hp.shape[1]
    rows = cap * LINES
    half = rows // 2
    order = row_count * rows
    parts = chip_count // row_count
    mask_rows = max(8, cap // 2)
    f32 = jnp.float32

    def device(r, m, k):
        return (r * chip_count + m) * 2 + k

    places = [
        (r, m, k) for r in range(row_count) for m in range(chip_count) for k in range(2)
    ]

    def send(value, target):
        pairs = []
        for r, m, k in places:
            to = target(r, m, k)
            if to is not None:
                pairs.append((device(r, m, k), device(*to)))
        return lax.ppermute(value, AXES, pairs)

    def to_other(value):
        return send(value, lambda r, m, k: (r, m, 1 - k))

    tiles = call(
        assemble_kernel,
        jax.ShapeDtypeStruct((3 * rows + mask_rows, LANES), f32),
        [VMEM] * 3 + [SMEM] * 8,
        [pltpu.VMEM((3, rows, LANES), f32), pltpu.SMEM((4 * cap,), jnp.int32)],
        1 << 20,
        hv, pv, sv, hp, pp, sp, xp, hc, pc, sc, xc,
    )
    other = to_other(tiles)
    ops = queues(row_count, chip_count)
    kinds = [tuple((item or op[1 - k])[0] for k, item in enumerate(op)) for op in ops]
    combos = sorted(set(kinds))
    packed = call(
        functools.partial(pack_kernel, rows, combos),
        [jax.ShapeDtypeStruct((rows, PAIR), f32) for _ in combos],
        [VMEM] * 2,
        [],
        1 << 20,
        tiles, other,
    )
    got, shared = [], []
    for op, kind in zip(ops, kinds):

        def target(r, m, k):
            if op[k] is None:
                return None
            matrix, offset = op[k]
            return (r, m ^ offset, k) if matrix == "H" else (r ^ offset, m, k)

        got.append(send(packed[combos.index(kind)], target))
        shared.append(to_other(got[-1]))

    def holding(matrices):
        return [i for i, op in enumerate(ops) if any(x and x[0] in matrices for x in op)]

    flops = 2 * 3 * half * order * PAIR
    splits = [pltpu.VMEM((order, PAIR), jnp.bfloat16)] * 2
    used = holding("HP")
    y = call(
        functools.partial(y_kernel, rows, [ops[i] for i in used]),
        jax.ShapeDtypeStruct((half, PAIR), f32),
        [VMEM] * (2 + 2 * len(used)),
        splits,
        flops,
        tiles, other, *[got[i] for i in used], *[shared[i] for i in used],
    )
    offsets = list(range(chip_count - 1, -1, -1))
    ys = [
        send(y, lambda r, m, k, o=o: (r, m ^ o, k)) if o else y
        for o in offsets
    ]
    used = holding("S")
    sent_shapes = [jax.ShapeDtypeStruct((LANES, PAIR), f32)] * (parts if parts > 1 else 0)
    x, swap, *sent = call(
        functools.partial(x_kernel, rows, [ops[i] for i in used], offsets, parts),
        [jax.ShapeDtypeStruct((half, PAIR), f32), jax.ShapeDtypeStruct((half, LANES), f32)]
        + sent_shapes,
        [VMEM] * (2 + 2 * len(used) + len(offsets)),
        splits,
        flops,
        tiles, other, *[got[i] for i in used], *[shared[i] for i in used], *ys,
    )
    sent = sent or [x]

    def mirror(turn):
        def target(r, m, k):
            part = (m % parts + turn) % parts
            column = (r * 2 * parts) + k * parts + part
            return m // parts, column // 2, column % 2

        return target

    mirrors = [send(value, mirror(turn)) for turn, value in enumerate(sent)]
    swapped = to_other(swap)
    return call(
        functools.partial(slots_kernel, parts),
        jax.ShapeDtypeStruct((1, cap, BS * BS), f32),
        [SMEM] * 2 + [VMEM] * (2 + parts),
        [
            pltpu.VMEM((rows, LANES), f32),
            pltpu.VMEM((rows, LANES), f32),
            pltpu.SMEM((cap,), jnp.int32),
        ],
        1 << 20,
        xp, xc, x, swapped, *mirrors,
    )


def solution(mesh):
    values, ints = P("row", "col", None), P("row", "col")
    row_count, col_count = mesh.shape["row"], mesh.shape["col"]
    return jax.shard_map(
        functools.partial(shards, row_count, col_count // 2),
        mesh=mesh,
        in_specs=(values, ints, ints) * 3 + (ints, ints),
        out_specs=values,
        check_vma=False,
    )
```

```python
import functools

import jax
import jax.numpy as jnp
from jax import lax
from jax.experimental import pallas as pl
from jax.experimental.pallas import tpu as pltpu
from jax.sharding import PartitionSpec as P

BS = 64
LANES = 128
COST = 1 << 10
LINES = BS * BS // LANES
VMEM = pl.BlockSpec(memory_space=pltpu.VMEM)
SMEM = pl.BlockSpec(memory_space=pltpu.SMEM)
AXES = ("row", "col")


def position():
    col = lax.axis_index("col")
    return lax.axis_index("row"), col // 2, col % 2


def left_lanes(rows):
    return lax.broadcasted_iota(jnp.int32, (rows, LANES), 1) < BS


def invert(places, inverse, base):
    cap = places.shape[1]
    for slot in range(cap):
        inverse[base + places[0, slot]] = slot


def fill(ref, rows):
    if ref.shape[0] > rows:
        ref[rows:, :] = jnp.zeros((ref.shape[0] - rows, LANES), jnp.float32)


def assemble(values, places, counts, lines, inverse, ready, tiles):
    left = left_lanes(LINES)
    for which, value in enumerate(values):
        cap = value.shape[1]
        ready(which)
        invert(places[which], inverse, which * cap)
        count = counts[which][0, 0]
        for line in range(LINES):
            lines[which, pl.ds(line, cap, stride=LINES), :] = value[
                0, :, line * LANES : (line + 1) * LANES
            ]

        def block(place):
            slot = inverse[which * cap + place]
            kept = (slot < count).astype(jnp.float32)
            start = pl.multiple_of(slot * LINES, LINES)
            return lines[which, pl.ds(start, LINES), :] * kept

        for pair in range(cap // 2):
            first, second = block(2 * pair), block(2 * pair + 1)
            even = jnp.where(left, first, pltpu.roll(second, BS, 1))
            odd = jnp.where(left, pltpu.roll(first, BS, 1), second)
            for tile in tiles[which]:
                tile[pl.ds(pair * BS, LINES, stride=2), :] = even
                tile[pl.ds(pair * BS + 1, LINES, stride=2), :] = odd
        for tile in tiles[which]:
            fill(tile, cap * LINES)


def first_kernel(value, places, count, near, far, value_in, places_in, lines, inverse, sems):
    copies = [
        pltpu.make_async_copy(places, places_in, sems.at[0]),
        pltpu.make_async_copy(value, value_in, sems.at[1]),
    ]
    for copy in copies:
        copy.start()

    def ready(_):
        for copy in copies:
            copy.wait()

    assemble([value_in], [places_in], [count], lines, inverse, ready, [(near, far)])


def rest_kernel(*refs):
    sources, counts, (h_tile, s_near, s_far, mask, order) = refs[:5], refs[5:8], refs[9:14]
    values, places = refs[14:16], refs[16:19]
    lines, inverse, sems = refs[19:]
    copies = [
        pltpu.make_async_copy(source, ref, sems.at[i])
        for i, (source, ref) in enumerate(zip(sources, refs[14:19]))
    ]
    for copy in copies:
        copy.start()
    cap = values[0].shape[1]

    def ready(which):
        copies[which].wait()
        copies[2 + which].wait()

    assemble(values, places, counts, lines, inverse, ready, [(h_tile,), (s_near, s_far)])
    copies[4].wait()
    invert(places[2], inverse, 2 * cap)
    count = counts[2][0, 0]
    slots = [inverse[2 * cap + place] for place in range(cap)]
    lanes = lax.broadcasted_iota(jnp.int32, (1, LANES), 1)
    row = jnp.where(lanes == cap, count, 0)
    for place in range(cap):
        row = jnp.where(lanes == place, slots[place], row)
    order[...] = row
    for pair in range(cap // 2):
        flags = [(slots[2 * pair + side] < count).astype(jnp.float32) for side in range(2)]
        mask[pair : pair + 1, :] = jnp.where(left_lanes(1), flags[0], flags[1])


def stack_kernel(others, count, rows, *refs):
    for i, ref in enumerate(refs[others : others + count]):
        refs[-1][i * rows : (i + 1) * rows, :] = ref[:rows, :]


def split(x):
    high = x.astype(jnp.bfloat16)
    return high, (x - high.astype(jnp.float32)).astype(jnp.bfloat16)


def dot3(a, b_high, b_low):
    a_high, a_low = split(a)
    dot = functools.partial(jnp.dot, preferred_element_type=jnp.float32)
    return dot(a_high, b_high) + (dot(a_high, b_low) + dot(a_low, b_high))


def product_kernel(along, across, sends, *refs):
    got, shared, b_own = refs[:3]
    b_got = refs[3 : 3 + len(along)]
    mask, out = refs[3 + len(along) :][:2]
    sent = refs[5 + len(along) : -2]
    high, low = refs[-2:]
    row, chip, core = position()
    rows = b_own.shape[0]
    for offset, ref in zip([0] + along, (b_own,) + b_got):
        at = pl.ds(pl.multiple_of((row ^ offset) * rows, rows), rows)
        high[at, :], low[at, :] = split(ref[:rows, :])
    acc = None
    for i, offset in enumerate([0] + across):
        for side in range(2):
            ref = (got, shared)[side]
            start = i * rows
            column = 2 * (chip ^ offset) + (core ^ side)
            at = pl.ds(pl.multiple_of(column * LANES, LANES), LANES)
            term = dot3(ref[start : start + rows, :], high[at, :], low[at, :])
            acc = term if acc is None else acc + term
    for pair in range(rows // BS):
        at = slice(pair * BS, (pair + 1) * BS)
        out[at, :] = acc[at, :] * mask[pair : pair + 1, :]
    fill(out, rows)
    for turn, ref in enumerate(sent):
        part = lax.rem(2 * chip + core + turn, sends)
        ref[...] = out[pl.ds(pl.multiple_of(part * LANES, LANES), LANES), :]


def slots_kernel(cap, order, x, *refs):
    mirrors, (out, tile, lines) = refs[:-3], refs[-3:]
    sends = len(mirrors)
    tile[...] = x[: tile.shape[0], :]
    for turn in range(sends):
        part = lax.rem(lax.axis_index("col") + (sends - turn), sends)
        at = pl.ds(pl.multiple_of(part * LANES, LANES), LANES)
        tile[at, :] += mirrors[turn][...].T
    count = order[0, cap]
    left = left_lanes(LINES)
    for pair in range(cap // 2):
        even = tile[pl.ds(pair * BS, LINES, stride=2), :]
        odd = tile[pl.ds(pair * BS + 1, LINES, stride=2), :]
        blocks = (
            jnp.where(left, even, pltpu.roll(odd, BS, 1)),
            jnp.where(left, pltpu.roll(even, BS, 1), odd),
        )
        for side in range(2):
            slot = order[0, 2 * pair + side]
            used = (slot < count).astype(jnp.float32)
            start = pl.multiple_of(slot * LINES, LINES)
            lines[pl.ds(start, LINES), :] = blocks[side] * used
    for line in range(LINES):
        out[0, :, line * LANES : (line + 1) * LANES] = lines[
            pl.ds(line, cap, stride=LINES), :
        ]


def call(kernel, out_shapes, in_specs, scratch, cost, *args):
    single = not isinstance(out_shapes, list)
    return pl.pallas_call(
        kernel,
        out_shape=out_shapes,
        in_specs=in_specs,
        out_specs=VMEM if single else [VMEM] * len(out_shapes),
        scratch_shapes=scratch,
        compiler_params=pltpu.CompilerParams(vmem_limit_bytes=32 * 1024 * 1024),
        cost_estimate=pl.CostEstimate(flops=COST, bytes_accessed=COST, transcendentals=0),
    )(*args)


def shards(row_count, chip_count, hv, hp, hc, pv, pp, pc, sv, sp, sc, xp, xc):
    cap = hp.shape[1]
    rows = cap * LINES
    order = row_count * rows
    sends = rows // LANES
    f32 = jnp.float32

    def device(r, m, k):
        return (r * chip_count + m) * 2 + k

    def send(value, target):
        pairs = [
            (device(r, m, k), device(*target(r, m, k)))
            for r in range(row_count)
            for m in range(chip_count)
            for k in range(2)
        ]
        return lax.ppermute(value, AXES, pairs)

    def to_other(value):
        return send(value, lambda r, m, k: (r, m, 1 - k))

    def stack(arrays, *others):
        return call(
            functools.partial(stack_kernel, len(others), len(arrays), rows),
            jax.ShapeDtypeStruct((len(arrays) * rows, LANES), f32),
            [pl.BlockSpec(memory_space=pl.ANY)] * len(others) + [VMEM] * len(arrays),
            [],
            1 << 10,
            *others, *arrays,
        )

    hv, hp, pv, pp, sv, sp, xp = (
        pltpu.with_memory_space_constraint(x, pltpu.HBM) for x in (hv, hp, pv, pp, sv, sp, xp)
    )
    hbm = pl.BlockSpec(memory_space=pltpu.HBM)
    value_in, places_in = pltpu.VMEM(hv.shape, f32), pltpu.SMEM(hp.shape, jnp.int32)
    tile, longer, longest = (
        jax.ShapeDtypeStruct((rows + 8 * extra, LANES), f32) for extra in range(3)
    )
    p_near, p_far = call(
        first_kernel,
        [tile, longest],
        [hbm, hbm, SMEM],
        [
            value_in,
            places_in,
            pltpu.VMEM((1, rows, LANES), f32),
            pltpu.SMEM((cap,), jnp.int32),
            pltpu.SemaphoreType.DMA((2,)),
        ],
        1 << 10,
        pv, pp, pc,
    )
    h_tile, s_near, s_far, mask, slot_order = call(
        rest_kernel,
        [
            longer,
            tile,
            longest,
            jax.ShapeDtypeStruct((max(8, cap // 2), LANES), f32),
            jax.ShapeDtypeStruct((1, LANES), jnp.int32),
        ],
        [hbm] * 5 + [SMEM] * 3 + [pl.BlockSpec(memory_space=pl.ANY)],
        [value_in] * 2
        + [places_in] * 3
        + [
            pltpu.VMEM((2, rows, LANES), f32),
            pltpu.SMEM((3 * cap,), jnp.int32),
            pltpu.SemaphoreType.DMA((5,)),
        ],
        1 << 10,
        hv, sv, hp, sp, xp, hc, sc, xc, p_near,
    )
    along = sorted(range(1, row_count), key=lambda s: (s != 1, s))
    across = list(range(chip_count - 1, 0, -1))

    def along_z(near, far):
        return [
            send(near if s == 1 else far, lambda r, m, k, s=s: (r ^ s, m, k)) for s in along
        ]

    def in_plane(x):
        return [send(x, lambda r, m, k, o=o: (r, m ^ o, k)) for o in across]

    def product(a_got, b, b_got, parts):
        part = jax.ShapeDtypeStruct((LANES, LANES), f32)
        return call(
            functools.partial(product_kernel, along, across, sends),
            [longer] + [part] * parts,
            [VMEM] * (4 + len(b_got)),
            [pltpu.VMEM((order, LANES), jnp.bfloat16)] * 2,
            2 * 3 * rows * order * LANES,
            a_got, to_other(a_got), b, *b_got, mask,
        )

    p_got = along_z(p_near, p_far)
    h_got = stack([h_tile] + in_plane(h_tile), *p_got)
    (y,) = product(h_got, p_near, p_got, 0)
    s_got = along_z(s_near, s_far)
    y_got = stack([y] + in_plane(y), *s_got)
    x, *sent = product(y_got, s_near, s_got, sends)

    def mirror(turn):
        def target(r, m, k):
            column = 2 * m + k
            part = (column + turn) % sends
            to = r * sends + part
            return column // sends, to // 2, to % 2

        return target

    mirrors = [send(value, mirror(turn)) for turn, value in enumerate(sent)]
    return call(
        functools.partial(slots_kernel, cap),
        jax.ShapeDtypeStruct((1, cap, BS * BS), f32),
        [SMEM] + [VMEM] * (1 + sends),
        [pltpu.VMEM((rows, LANES), f32)] * 2,
        1 << 20,
        slot_order, x, *mirrors,
    )


def solution(mesh):
    values, ints = P("row", "col", None), P("row", "col")
    row_count, col_count = mesh.shape["row"], mesh.shape["col"]
    return jax.shard_map(
        functools.partial(shards, row_count, col_count // 2),
        mesh=mesh,
        in_specs=(values, ints, ints) * 3 + (ints, ints),
        out_specs=values,
        check_vma=False,
    )
```

```python
import functools

import jax
import jax.numpy as jnp
from jax import lax
from jax.experimental import pallas as pl
from jax.experimental.pallas import tpu as pltpu
from jax.sharding import PartitionSpec as P

BS = 64
LANES = 128
COST = 1 << 10
LINES = BS * BS // LANES
VMEM = pl.BlockSpec(memory_space=pltpu.VMEM)
SMEM = pl.BlockSpec(memory_space=pltpu.SMEM)
AXES = ("row", "col")


def position():
    col = lax.axis_index("col")
    return lax.axis_index("row"), col // 2, col % 2


def left_lanes(rows):
    return lax.broadcasted_iota(jnp.int32, (rows, LANES), 1) < BS


def invert(places, inverse, base):
    cap = places.shape[1]
    for slot in range(cap):
        inverse[base + places[0, slot]] = slot


def fill(ref, rows):
    if ref.shape[0] > rows:
        ref[rows:, :] = jnp.zeros((ref.shape[0] - rows, LANES), jnp.float32)


def assemble(values, places, counts, lines, inverse, ready, tiles):
    left = left_lanes(LINES)
    for which, value in enumerate(values):
        cap = value.shape[1]
        ready(which)
        invert(places[which], inverse, which * cap)
        count = counts[which][0, 0]
        for line in range(LINES):
            lines[which, pl.ds(line, cap, stride=LINES), :] = value[
                0, :, line * LANES : (line + 1) * LANES
            ]

        def block(place):
            slot = inverse[which * cap + place]
            kept = (slot < count).astype(jnp.float32)
            start = pl.multiple_of(slot * LINES, LINES)
            return lines[which, pl.ds(start, LINES), :] * kept

        for pair in range(cap // 2):
            first, second = block(2 * pair), block(2 * pair + 1)
            even = jnp.where(left, first, pltpu.roll(second, BS, 1))
            odd = jnp.where(left, pltpu.roll(first, BS, 1), second)
            for tile in tiles[which]:
                tile[pl.ds(pair * BS, LINES, stride=2), :] = even
                tile[pl.ds(pair * BS + 1, LINES, stride=2), :] = odd
        for tile in tiles[which]:
            fill(tile, cap * LINES)


def first_kernel(value, places, count, near, far, value_in, places_in, lines, inverse, sems):
    copies = [
        pltpu.make_async_copy(places, places_in, sems.at[0]),
        pltpu.make_async_copy(value, value_in, sems.at[1]),
    ]
    for copy in copies:
        copy.start()

    def ready(_):
        for copy in copies:
            copy.wait()

    assemble([value_in], [places_in], [count], lines, inverse, ready, [(near, far)])


def rest_kernel(*refs):
    sources, counts, (h_tile, s_near, s_far, mask, order) = refs[:5], refs[5:8], refs[9:14]
    values, places = refs[14:16], refs[16:19]
    lines, inverse, sems = refs[19:]
    copies = [
        pltpu.make_async_copy(source, ref, sems.at[i])
        for i, (source, ref) in enumerate(zip(sources, refs[14:19]))
    ]
    for copy in copies:
        copy.start()
    cap = values[0].shape[1]

    def ready(which):
        copies[which].wait()
        copies[2 + which].wait()

    assemble(values, places, counts, lines, inverse, ready, [(h_tile,), (s_near, s_far)])
    copies[4].wait()
    invert(places[2], inverse, 2 * cap)
    count = counts[2][0, 0]
    slots = [inverse[2 * cap + place] for place in range(cap)]
    lanes = lax.broadcasted_iota(jnp.int32, (1, LANES), 1)
    row = jnp.where(lanes == cap, count, 0)
    for place in range(cap):
        row = jnp.where(lanes == place, slots[place], row)
    order[...] = row
    for pair in range(cap // 2):
        flags = [(slots[2 * pair + side] < count).astype(jnp.float32) for side in range(2)]
        mask[pair : pair + 1, :] = jnp.where(left_lanes(1), flags[0], flags[1])


def stack_kernel(others, count, rows, *refs):
    for i, ref in enumerate(refs[others : others + count]):
        refs[-1][i * rows : (i + 1) * rows, :] = ref[:rows, :]


def split(x):
    high = x.astype(jnp.bfloat16)
    return high, (x - high.astype(jnp.float32)).astype(jnp.bfloat16)


def dot3(a, b_high, b_low):
    a_high, a_low = split(a)
    dot = functools.partial(jnp.dot, preferred_element_type=jnp.float32)
    return dot(a_high, b_high) + (dot(a_high, b_low) + dot(a_low, b_high))


def product_kernel(along, across, sends, *refs):
    got, shared, b_own = refs[:3]
    b_got = refs[3 : 3 + len(along)]
    mask, out = refs[3 + len(along) :][:2]
    sent = refs[5 + len(along) : -2]
    high, low = refs[-2:]
    row, chip, core = position()
    rows = b_own.shape[0]
    for offset, ref in zip([0] + along, (b_own,) + b_got):
        at = pl.ds(pl.multiple_of((row ^ offset) * rows, rows), rows)
        high[at, :], low[at, :] = split(ref[:rows, :])
    acc = None
    for i, offset in enumerate([0] + across):
        for side in range(2):
            ref = (got, shared)[side]
            start = i * rows
            column = 2 * (chip ^ offset) + (core ^ side)
            at = pl.ds(pl.multiple_of(column * LANES, LANES), LANES)
            term = dot3(ref[start : start + rows, :], high[at, :], low[at, :])
            acc = term if acc is None else acc + term
    for pair in range(rows // BS):
        at = slice(pair * BS, (pair + 1) * BS)
        out[at, :] = acc[at, :] * mask[pair : pair + 1, :]
    fill(out, rows)
    for turn, ref in enumerate(sent):
        part = lax.rem(2 * chip + core + turn, sends)
        ref[...] = out[pl.ds(pl.multiple_of(part * LANES, LANES), LANES), :]


def slots_kernel(cap, sends, order, x, *refs):
    mirrors, (out, tile, lines) = refs[:-3], refs[-3:]
    row, chip, _ = position()
    tile[...] = x[: tile.shape[0], :]

    def add(parts):
        for turn, value in enumerate(parts):
            part = lax.rem(lax.axis_index("col") + (sends - turn), sends)
            at = pl.ds(pl.multiple_of(part * LANES, LANES), LANES)
            tile[at, :] += value.T

    def straight():
        add([ref[...] for ref in mirrors[:sends]])

    if len(mirrors) == sends:
        straight()
    else:
        kept, other = mirrors[2 * sends :]
        far = row ^ chip
        pl.when(far == 0)(lambda: add([kept[...], other[...]]))
        pl.when(far == 1)(lambda: add([ref[...] for ref in mirrors[sends : 2 * sends]]))
        pl.when(far > 1)(straight)
    count = order[0, cap]
    left = left_lanes(LINES)
    for pair in range(cap // 2):
        even = tile[pl.ds(pair * BS, LINES, stride=2), :]
        odd = tile[pl.ds(pair * BS + 1, LINES, stride=2), :]
        blocks = (
            jnp.where(left, even, pltpu.roll(odd, BS, 1)),
            jnp.where(left, pltpu.roll(even, BS, 1), odd),
        )
        for side in range(2):
            slot = order[0, 2 * pair + side]
            used = (slot < count).astype(jnp.float32)
            start = pl.multiple_of(slot * LINES, LINES)
            lines[pl.ds(start, LINES), :] = blocks[side] * used
    for line in range(LINES):
        out[0, :, line * LANES : (line + 1) * LANES] = lines[
            pl.ds(line, cap, stride=LINES), :
        ]


def call(kernel, out_shapes, in_specs, scratch, cost, *args):
    single = not isinstance(out_shapes, list)
    return pl.pallas_call(
        kernel,
        out_shape=out_shapes,
        in_specs=in_specs,
        out_specs=VMEM if single else [VMEM] * len(out_shapes),
        scratch_shapes=scratch,
        compiler_params=pltpu.CompilerParams(vmem_limit_bytes=32 * 1024 * 1024),
        cost_estimate=pl.CostEstimate(flops=COST, bytes_accessed=COST, transcendentals=0),
    )(*args)


def shards(row_count, chip_count, hv, hp, hc, pv, pp, pc, sv, sp, sc, xp, xc):
    cap = hp.shape[1]
    rows = cap * LINES
    order = row_count * rows
    sends = rows // LANES
    f32 = jnp.float32

    def device(r, m, k):
        return (r * chip_count + m) * 2 + k

    def send(value, target):
        pairs = [
            (device(r, m, k), device(*target(r, m, k)))
            for r in range(row_count)
            for m in range(chip_count)
            for k in range(2)
            if target(r, m, k)
        ]
        return lax.ppermute(value, AXES, pairs)

    def to_other(value):
        return send(value, lambda r, m, k: (r, m, 1 - k))

    def stack(arrays, *others):
        return call(
            functools.partial(stack_kernel, len(others), len(arrays), rows),
            jax.ShapeDtypeStruct((len(arrays) * rows, LANES), f32),
            [pl.BlockSpec(memory_space=pl.ANY)] * len(others) + [VMEM] * len(arrays),
            [],
            1 << 10,
            *others, *arrays,
        )

    hv, hp, pv, pp, sv, sp, xp = (
        pltpu.with_memory_space_constraint(x, pltpu.HBM) for x in (hv, hp, pv, pp, sv, sp, xp)
    )
    hbm = pl.BlockSpec(memory_space=pltpu.HBM)
    value_in, places_in = pltpu.VMEM(hv.shape, f32), pltpu.SMEM(hp.shape, jnp.int32)
    tile, longer, longest = (
        jax.ShapeDtypeStruct((rows + 8 * extra, LANES), f32) for extra in range(3)
    )
    p_near, p_far = call(
        first_kernel,
        [tile, longest],
        [hbm, hbm, SMEM],
        [
            value_in,
            places_in,
            pltpu.VMEM((1, rows, LANES), f32),
            pltpu.SMEM((cap,), jnp.int32),
            pltpu.SemaphoreType.DMA((2,)),
        ],
        1 << 10,
        pv, pp, pc,
    )
    h_tile, s_near, s_far, mask, slot_order = call(
        rest_kernel,
        [
            longer,
            tile,
            longest,
            jax.ShapeDtypeStruct((max(8, cap // 2), LANES), f32),
            jax.ShapeDtypeStruct((1, LANES), jnp.int32),
        ],
        [hbm] * 5 + [SMEM] * 3 + [pl.BlockSpec(memory_space=pl.ANY)],
        [value_in] * 2
        + [places_in] * 3
        + [
            pltpu.VMEM((2, rows, LANES), f32),
            pltpu.SMEM((3 * cap,), jnp.int32),
            pltpu.SemaphoreType.DMA((5,)),
        ],
        1 << 10,
        hv, sv, hp, sp, xp, hc, sc, xc, p_near,
    )
    along = list(range(row_count - 1, 0, -1))
    across = list(range(chip_count - 1, 0, -1))

    def along_z(near, far):
        got = {}
        for offset in sorted(along, key=lambda s: s.bit_count()):
            low = offset & -offset
            if offset != low:
                value = stack([got[offset ^ low]])
            else:
                value = near if low == 1 else far
            got[offset] = send(value, lambda r, m, k: (r ^ low, m, k))
        return [got[offset] for offset in along]

    def in_plane(x):
        return [send(x, lambda r, m, k, o=o: (r, m ^ o, k)) for o in across]

    def product(a_got, b, b_got, parts):
        part = jax.ShapeDtypeStruct((LANES, LANES), f32)
        return call(
            functools.partial(product_kernel, along, across, sends),
            [longer] + [part] * parts,
            [VMEM] * (4 + len(b_got)),
            [pltpu.VMEM((order, LANES), jnp.bfloat16)] * 2,
            2 * 3 * rows * order * LANES,
            a_got, to_other(a_got), b, *b_got, mask,
        )

    p_got = along_z(p_far, p_far)
    h_got = stack([h_tile] + in_plane(h_tile), *p_got)
    (y,) = product(h_got, p_near, p_got, 0)
    s_got = along_z(s_near, s_far)
    y_got = stack([y] + in_plane(y), *s_got)
    x, *sent = product(y_got, s_near, s_got, sends)

    relay = row_count == chip_count == 4

    def mirror(turn):
        def target(r, m, k):
            column = 2 * m + k
            part = (column + turn) % sends
            if relay and r ^ m < 2:
                return r, m ^ 1, part
            to = r * sends + part
            return column // sends, to // 2, to % 2

        return target

    mirrors = [send(value, mirror(turn)) for turn, value in enumerate(sent)]
    if relay:
        mirrors += [
            *(
                send(part, lambda r, m, k: (r ^ 1, m, k) if r == m else None)
                for part in mirrors
            ),
            sent[0],
            to_other(sent[1]),
        ]
    return call(
        functools.partial(slots_kernel, cap, sends),
        jax.ShapeDtypeStruct((1, cap, BS * BS), f32),
        [SMEM] + [VMEM] * (1 + len(mirrors)),
        [pltpu.VMEM((rows, LANES), f32)] * 2,
        1 << 20,
        slot_order, x, *mirrors,
    )


def solution(mesh):
    values, ints = P("row", "col", None), P("row", "col")
    row_count, col_count = mesh.shape["row"], mesh.shape["col"]
    return jax.shard_map(
        functools.partial(shards, row_count, col_count // 2),
        mesh=mesh,
        in_specs=(values, ints, ints) * 3 + (ints, ints),
        out_specs=values,
        check_vma=False,
    )
```

```python
import functools

import jax
import jax.numpy as jnp
from jax import lax
from jax.experimental import pallas as pl
from jax.experimental.pallas import tpu as pltpu
from jax.sharding import PartitionSpec as P

BS = 64
LANES = 128
COST = 1 << 10
LINES = BS * BS // LANES
VMEM = pl.BlockSpec(memory_space=pltpu.VMEM)
SMEM = pl.BlockSpec(memory_space=pltpu.SMEM)
AXES = ("row", "col")


def position():
    col = lax.axis_index("col")
    return lax.axis_index("row"), col // 2, col % 2


def left_lanes(rows):
    return lax.broadcasted_iota(jnp.int32, (rows, LANES), 1) < BS


def slot_places(places, count, rows=LINES):
    return [
        jnp.where(slot < count, jnp.broadcast_to(places[0:1, slot : slot + 1], (rows, LANES)), -1)
        for slot in range(places.shape[1])
    ]


def fill(ref, rows):
    if ref.shape[0] > rows:
        ref[rows:, :] = jnp.zeros((ref.shape[0] - rows, LANES), jnp.float32)


def assemble(value, places, count, lines, tiles):
    left = left_lanes(LINES)
    cap = value.shape[1]
    for line in range(LINES):
        lines[pl.ds(line, cap, stride=LINES), :] = value[0, :, line * LANES : (line + 1) * LANES]
    at = slot_places(places, count)

    def block(place):
        picked = jnp.zeros((LINES, LANES), jnp.float32)
        for slot in range(cap):
            rows = lines[slot * LINES : (slot + 1) * LINES, :]
            picked = jnp.where(at[slot] == place, rows, picked)
        return picked

    for pair in range(cap // 2):
        first, second = block(2 * pair), block(2 * pair + 1)
        even = jnp.where(left, first, pltpu.roll(second, BS, 1))
        odd = jnp.where(left, pltpu.roll(first, BS, 1), second)
        for tile in tiles:
            tile[pl.ds(pair * BS, LINES, stride=2), :] = even
            tile[pl.ds(pair * BS + 1, LINES, stride=2), :] = odd
    for tile in tiles:
        fill(tile, cap * LINES)


def first_kernel(count, *refs):
    sources, (near, far), fetched = refs[:7], refs[7:9], refs[9:14]
    value_in, places_in, lines, sems = refs[14:]
    copies = [
        pltpu.make_async_copy(source, ref, sems.at[i])
        for i, (source, ref) in enumerate(zip(sources, (places_in, value_in) + fetched))
    ]
    for copy in copies:
        copy.start()
    for copy in copies[:2]:
        copy.wait()
    assemble(value_in, places_in, count[0, 0], lines, (near, far))
    for copy in copies[2:]:
        copy.wait()


def rest_kernel(hv, sv, hp, sp, xp, hc, sc, xc, h_tile, s_near, s_far, mask, lines):
    assemble(hv, hp, hc[0, 0], lines, (h_tile,))
    assemble(sv, sp, sc[0, 0], lines, (s_near, s_far))
    cap = xp.shape[1]
    at = slot_places(xp, xc[0, 0], 1)

    def flag(place):
        present = jnp.zeros((1, LANES), jnp.float32)
        for slot in range(cap):
            present = jnp.where(at[slot] == place, 1.0, present)
        return present

    for pair in range(cap // 2):
        mask[pair : pair + 1, :] = jnp.where(left_lanes(1), flag(2 * pair), flag(2 * pair + 1))


def stack_kernel(others, count, rows, *refs):
    for i, ref in enumerate(refs[others : others + count]):
        refs[-1][i * rows : (i + 1) * rows, :] = ref[:rows, :]


def split(x):
    high = x.astype(jnp.bfloat16)
    return high, (x - high.astype(jnp.float32)).astype(jnp.bfloat16)


def dot3(a, b_high, b_low):
    a_high, a_low = split(a)
    dot = functools.partial(jnp.dot, preferred_element_type=jnp.float32)
    return dot(a_high, b_high) + (dot(a_high, b_low) + dot(a_low, b_high))


def product_kernel(along, across, sends, *refs):
    got, shared, b_own = refs[:3]
    b_got = refs[3 : 3 + len(along)]
    mask, out = refs[3 + len(along) :][:2]
    sent = refs[5 + len(along) : -2]
    high, low = refs[-2:]
    row, chip, core = position()
    rows = b_own.shape[0]
    for offset, ref in zip([0] + along, (b_own,) + b_got):
        at = pl.ds(pl.multiple_of((row ^ offset) * rows, rows), rows)
        high[at, :], low[at, :] = split(ref[:rows, :])
    acc = None
    for i, offset in enumerate([0] + across):
        for side in range(2):
            ref = (got, shared)[side]
            start = i * rows
            column = 2 * (chip ^ offset) + (core ^ side)
            at = pl.ds(pl.multiple_of(column * LANES, LANES), LANES)
            term = dot3(ref[start : start + rows, :], high[at, :], low[at, :])
            acc = term if acc is None else acc + term
    for pair in range(rows // BS):
        at = slice(pair * BS, (pair + 1) * BS)
        out[at, :] = acc[at, :] * mask[pair : pair + 1, :]
    fill(out, rows)
    for turn, ref in enumerate(sent):
        part = lax.rem(2 * chip + core + turn, sends)
        ref[...] = out[pl.ds(pl.multiple_of(part * LANES, LANES), LANES), :]


def slots_kernel(cap, sends, places, count, x, *refs):
    mirrors, (out, tile, lines) = refs[:-3], refs[-3:]
    row, chip, _ = position()
    tile[...] = x[: tile.shape[0], :]

    def add(parts):
        for turn, value in enumerate(parts):
            part = lax.rem(lax.axis_index("col") + (sends - turn), sends)
            at = pl.ds(pl.multiple_of(part * LANES, LANES), LANES)
            tile[at, :] += value.T

    def straight():
        add([ref[...] for ref in mirrors[:sends]])

    if len(mirrors) == sends:
        straight()
    else:
        relayed, kept, other = (ref[...] for ref in mirrors[sends:])
        far = row ^ chip
        pl.when(far == 0)(lambda: add([kept, other]))
        pl.when(far == 1)(lambda: add([relayed, mirrors[1][...]]))
        pl.when(far > 1)(straight)
    left = left_lanes(LINES)
    blocks = []
    for pair in range(cap // 2):
        even = tile[pl.ds(pair * BS, LINES, stride=2), :]
        odd = tile[pl.ds(pair * BS + 1, LINES, stride=2), :]
        blocks.append(jnp.where(left, even, pltpu.roll(odd, BS, 1)))
        blocks.append(jnp.where(left, pltpu.roll(even, BS, 1), odd))
    for slot, at in enumerate(slot_places(places, count[0, 0])):
        picked = jnp.zeros((LINES, LANES), jnp.float32)
        for place, block in enumerate(blocks):
            picked = jnp.where(at == place, block, picked)
        lines[slot * LINES : (slot + 1) * LINES, :] = picked
    for line in range(LINES):
        out[0, :, line * LANES : (line + 1) * LANES] = lines[
            pl.ds(line, cap, stride=LINES), :
        ]


def call(kernel, out_shapes, in_specs, scratch, cost, *args):
    single = not isinstance(out_shapes, list)
    return pl.pallas_call(
        kernel,
        out_shape=out_shapes,
        in_specs=in_specs,
        out_specs=VMEM if single else [VMEM] * len(out_shapes),
        scratch_shapes=scratch,
        compiler_params=pltpu.CompilerParams(vmem_limit_bytes=32 * 1024 * 1024),
        cost_estimate=pl.CostEstimate(flops=COST, bytes_accessed=COST, transcendentals=0),
    )(*args)


def shards(row_count, chip_count, hv, hp, hc, pv, pp, pc, sv, sp, sc, xp, xc):
    cap = hp.shape[1]
    rows = cap * LINES
    order = row_count * rows
    sends = rows // LANES
    f32 = jnp.float32

    def device(r, m, k):
        return (r * chip_count + m) * 2 + k

    def send(value, target):
        pairs = [
            (device(r, m, k), device(*target(r, m, k)))
            for r in range(row_count)
            for m in range(chip_count)
            for k in range(2)
            if target(r, m, k)
        ]
        return lax.ppermute(value, AXES, pairs)

    def to_other(value):
        return send(value, lambda r, m, k: (r, m, 1 - k))

    def stack(arrays, *others):
        return call(
            functools.partial(stack_kernel, len(others), len(arrays), rows),
            jax.ShapeDtypeStruct((len(arrays) * rows, LANES), f32),
            [pl.BlockSpec(memory_space=pl.ANY)] * len(others) + [VMEM] * len(arrays),
            [],
            1 << 10,
            *others, *arrays,
        )

    inputs = [
        pltpu.with_memory_space_constraint(x, pltpu.HBM) for x in (pp, pv, hv, sv, hp, sp, xp)
    ]
    tile, longer, longest = (
        jax.ShapeDtypeStruct((rows + 8 * extra, LANES), f32) for extra in range(3)
    )
    lines = pltpu.VMEM((rows, LANES), f32)
    p_near, p_far, hv, sv, hp, sp, xp = call(
        first_kernel,
        [tile, longest] + [jax.ShapeDtypeStruct(x.shape, x.dtype) for x in inputs[2:]],
        [SMEM] + [pl.BlockSpec(memory_space=pltpu.HBM)] * 7,
        [
            pltpu.VMEM(pv.shape, f32),
            pltpu.VMEM(pp.shape, jnp.int32),
            lines,
            pltpu.SemaphoreType.DMA((7,)),
        ],
        1 << 10,
        pc, *inputs,
    )
    h_tile, s_near, s_far, mask = call(
        rest_kernel,
        [longer, tile, longest, jax.ShapeDtypeStruct((max(8, cap // 2), LANES), f32)],
        [VMEM] * 5 + [SMEM] * 3,
        [lines],
        1 << 10,
        hv, sv, hp, sp, xp, hc, sc, xc,
    )
    along = list(range(row_count - 1, 0, -1))
    across = list(range(chip_count - 1, 0, -1))

    def along_z(near, far):
        got = {}
        for offset in sorted(along, key=lambda s: s.bit_count()):
            low = offset & -offset
            if offset != low:
                value = stack([got[offset ^ low]])
            else:
                value = near if low == 1 else far
            got[offset] = send(value, lambda r, m, k: (r ^ low, m, k))
        return [got[offset] for offset in along]

    def in_plane(x):
        return [send(x, lambda r, m, k, o=o: (r, m ^ o, k)) for o in across]

    def product(a_got, b, b_got, parts):
        part = jax.ShapeDtypeStruct((LANES, LANES), f32)
        return call(
            functools.partial(product_kernel, along, across, sends),
            [longer] + [part] * parts,
            [VMEM] * (4 + len(b_got)),
            [pltpu.VMEM((order, LANES), jnp.bfloat16)] * 2,
            2 * 3 * rows * order * LANES,
            a_got, to_other(a_got), b, *b_got, mask,
        )

    p_got = along_z(p_far, p_far)
    h_got = stack([h_tile] + in_plane(h_tile), *p_got)
    (y,) = product(h_got, p_near, p_got, 0)
    s_got = along_z(s_near, s_far)
    y_got = stack([y] + in_plane(y), *s_got)
    x, *sent = product(y_got, s_near, s_got, sends)

    relay = row_count == chip_count == 4

    def mirror(turn):
        def target(r, m, k):
            column = 2 * m + k
            part = (column + turn) % sends
            if relay and turn == 0 and r ^ m < 2:
                return r, m ^ 1, part
            to = r * sends + part
            return column // sends, to // 2, to % 2

        return target

    mirrors = [send(value, mirror(turn)) for turn, value in enumerate(sent)]
    if relay:
        mirrors += [
            send(mirrors[0], lambda r, m, k: (r ^ 1, m, k) if r == m else None),
            sent[0],
            to_other(sent[1]),
        ]
    return call(
        functools.partial(slots_kernel, cap, sends),
        jax.ShapeDtypeStruct((1, cap, BS * BS), f32),
        [VMEM, SMEM] + [VMEM] * (1 + len(mirrors)),
        [lines] * 2,
        1 << 20,
        xp, xc, x, *mirrors,
    )


def solution(mesh):
    values, ints = P("row", "col", None), P("row", "col")
    row_count, col_count = mesh.shape["row"], mesh.shape["col"]
    return jax.shard_map(
        functools.partial(shards, row_count, col_count // 2),
        mesh=mesh,
        in_specs=(values, ints, ints) * 3 + (ints, ints),
        out_specs=values,
        check_vma=False,
    )
```

```python
import functools

import jax
import jax.numpy as jnp
from jax import lax
from jax.experimental import pallas as pl
from jax.experimental.pallas import tpu as pltpu
from jax.sharding import PartitionSpec as P

BS = 64
LANES = 128
COST = 1 << 10
LINES = BS * BS // LANES
VMEM = pl.BlockSpec(memory_space=pltpu.VMEM)
SMEM = pl.BlockSpec(memory_space=pltpu.SMEM)
AXES = ("row", "col")


def position():
    col = lax.axis_index("col")
    return lax.axis_index("row"), col // 2, col % 2


def left_lanes(rows):
    return lax.broadcasted_iota(jnp.int32, (rows, LANES), 1) < BS


def slot_places(places, count, rows=LINES):
    return [
        jnp.where(slot < count, jnp.broadcast_to(places[0:1, slot : slot + 1], (rows, LANES)), -1)
        for slot in range(places.shape[1])
    ]


def fill(ref, rows):
    if ref.shape[0] > rows:
        ref[rows:, :] = jnp.zeros((ref.shape[0] - rows, LANES), jnp.float32)


def assemble(value, places, count, lines, tiles):
    left = left_lanes(LINES)
    cap = value.shape[1]
    for line in range(LINES):
        lines[pl.ds(line, cap, stride=LINES), :] = value[0, :, line * LANES : (line + 1) * LANES]
    at = slot_places(places, count)

    def block(place):
        picked = jnp.zeros((LINES, LANES), jnp.float32)
        for slot in range(cap):
            rows = lines[slot * LINES : (slot + 1) * LINES, :]
            picked = jnp.where(at[slot] == place, rows, picked)
        return picked

    for pair in range(cap // 2):
        first, second = block(2 * pair), block(2 * pair + 1)
        even = jnp.where(left, first, pltpu.roll(second, BS, 1))
        odd = jnp.where(left, pltpu.roll(first, BS, 1), second)
        for tile in tiles:
            tile[pl.ds(pair * BS, LINES, stride=2), :] = even
            tile[pl.ds(pair * BS + 1, LINES, stride=2), :] = odd
    for tile in tiles:
        fill(tile, cap * LINES)


def first_kernel(count, *refs):
    sources, (near, far), fetched = refs[:7], refs[7:9], refs[9:14]
    value_in, places_in, lines, sems = refs[14:]
    copies = [
        pltpu.make_async_copy(source, ref, sems.at[i])
        for i, (source, ref) in enumerate(zip(sources, (places_in, value_in) + fetched))
    ]
    for copy in copies:
        copy.start()
    for copy in copies[:2]:
        copy.wait()
    assemble(value_in, places_in, count[0, 0], lines, (near, far))
    for copy in copies[2:]:
        copy.wait()


def rest_kernel(hv, sv, hp, sp, xp, hc, sc, xc, h_tile, s_near, s_far, mask, lines):
    assemble(hv, hp, hc[0, 0], lines, (h_tile,))
    assemble(sv, sp, sc[0, 0], lines, (s_near, s_far))
    cap = xp.shape[1]
    at = slot_places(xp, xc[0, 0], 1)

    def flag(place):
        present = jnp.zeros((1, LANES), jnp.float32)
        for slot in range(cap):
            present = jnp.where(at[slot] == place, 1.0, present)
        return present

    for pair in range(cap // 2):
        mask[pair : pair + 1, :] = jnp.where(left_lanes(1), flag(2 * pair), flag(2 * pair + 1))


def stack_kernel(others, count, rows, *refs):
    for i, ref in enumerate(refs[others : others + count]):
        refs[-1][i * rows : (i + 1) * rows, :] = ref[:rows, :]


def parted_kernel(x, *outs):
    rows = outs[0].shape[0]
    for i, out in enumerate(outs):
        out[...] = x[i * rows : (i + 1) * rows, :]


def split(x):
    high = x.astype(jnp.bfloat16)
    return high, (x - high.astype(jnp.float32)).astype(jnp.bfloat16)


def product_kernel(along, across, shares, waits, *refs):
    got, shared, b_own = refs[0], refs[1 : 1 + shares], refs[1 + shares]
    refs = refs[2 + shares :]
    b_got, mask, out = refs[: len(along)], refs[len(along)], refs[len(along) + 1 + waits]
    sent, both = refs[len(along) + 2 + waits : -1], refs[-1]
    row, chip, core = position()
    rows = b_own.shape[0]
    for offset, ref in zip([0] + along, (b_own,) + b_got):
        at = pl.ds(pl.multiple_of((row ^ offset) * rows, rows), rows)
        both[at, :LANES], both[at, LANES:] = split(ref[:rows, :])
    dot = functools.partial(jnp.dot, preferred_element_type=jnp.float32)

    def multiply(left, right):
        wide, narrow = None, None

        def piece(refs, i):
            per = (1 + len(across)) // len(refs)
            return refs[i // per][i % per * rows : (i % per + 1) * rows, :]

        for i, offset in enumerate([0] + across):
            at = pl.ds(pl.multiple_of((chip ^ offset) * 2 * LANES, 2 * LANES), 2 * LANES)
            a = jnp.concatenate([piece(left, i), piece(right, i)], axis=1)
            a_high, a_low = split(a)
            terms = dot(a_high, both[at, :]), dot(a_low, both[at, :LANES])
            wide = terms[0] if wide is None else wide + terms[0]
            narrow = terms[1] if narrow is None else narrow + terms[1]
        acc = wide[:, :LANES] + (wide[:, LANES:] + narrow)
        for pair in range(rows // BS):
            at = slice(pair * BS, (pair + 1) * BS)
            out[at, :] = acc[at, :] * mask[pair : pair + 1, :]

    pl.when(core == 0)(lambda: multiply([got], shared))
    pl.when(core == 1)(lambda: multiply(shared, [got]))
    fill(out, rows)
    for turn, ref in enumerate(sent):
        part = lax.rem(2 * chip + core + turn, len(sent))
        ref[...] = out[pl.ds(pl.multiple_of(part * LANES, LANES), LANES), :]


def slots_kernel(cap, sends, places, count, x, *refs):
    mirrors, (out, tile, lines) = refs[:-3], refs[-3:]
    row, chip, _ = position()
    tile[...] = x[: tile.shape[0], :]

    def add(parts):
        for turn, value in enumerate(parts):
            part = lax.rem(lax.axis_index("col") + (sends - turn), sends)
            at = pl.ds(pl.multiple_of(part * LANES, LANES), LANES)
            tile[at, :] += value.T

    def straight():
        add([ref[...] for ref in mirrors[:sends]])

    if len(mirrors) == sends:
        straight()
    else:
        relayed, kept, other = (ref[...] for ref in mirrors[sends:])
        far = row ^ chip
        pl.when(far == 0)(lambda: add([kept, other]))
        pl.when(far == 1)(lambda: add([relayed, mirrors[1][...]]))
        pl.when(far > 1)(straight)
    left = left_lanes(LINES)
    blocks = []
    for pair in range(cap // 2):
        even = tile[pl.ds(pair * BS, LINES, stride=2), :]
        odd = tile[pl.ds(pair * BS + 1, LINES, stride=2), :]
        blocks.append(jnp.where(left, even, pltpu.roll(odd, BS, 1)))
        blocks.append(jnp.where(left, pltpu.roll(even, BS, 1), odd))
    for slot, at in enumerate(slot_places(places, count[0, 0])):
        picked = jnp.zeros((LINES, LANES), jnp.float32)
        for place, block in enumerate(blocks):
            picked = jnp.where(at == place, block, picked)
        lines[slot * LINES : (slot + 1) * LINES, :] = picked
    for line in range(LINES):
        out[0, :, line * LANES : (line + 1) * LANES] = lines[
            pl.ds(line, cap, stride=LINES), :
        ]


def call(kernel, out_shapes, in_specs, scratch, cost, *args):
    single = not isinstance(out_shapes, list)
    return pl.pallas_call(
        kernel,
        out_shape=out_shapes,
        in_specs=in_specs,
        out_specs=VMEM if single else [VMEM] * len(out_shapes),
        scratch_shapes=scratch,
        compiler_params=pltpu.CompilerParams(vmem_limit_bytes=32 * 1024 * 1024),
        cost_estimate=pl.CostEstimate(flops=COST, bytes_accessed=COST, transcendentals=0),
    )(*args)


def shards(row_count, chip_count, hv, hp, hc, pv, pp, pc, sv, sp, sc, xp, xc):
    cap = hp.shape[1]
    rows = cap * LINES
    order = row_count * rows
    sends = rows // LANES
    f32 = jnp.float32

    def device(r, m, k):
        return (r * chip_count + m) * 2 + k

    def send(value, target):
        pairs = [
            (device(r, m, k), device(*target(r, m, k)))
            for r in range(row_count)
            for m in range(chip_count)
            for k in range(2)
            if target(r, m, k)
        ]
        return lax.ppermute(value, AXES, pairs)

    def to_other(value):
        return send(value, lambda r, m, k: (r, m, 1 - k))

    def stack(arrays, *others):
        return call(
            functools.partial(stack_kernel, len(others), len(arrays), rows),
            jax.ShapeDtypeStruct((len(arrays) * rows, LANES), f32),
            [pl.BlockSpec(memory_space=pl.ANY)] * len(others) + [VMEM] * len(arrays),
            [],
            1 << 10,
            *others, *arrays,
        )

    inputs = [
        pltpu.with_memory_space_constraint(x, pltpu.HBM) for x in (pp, pv, hv, sv, hp, sp, xp)
    ]
    tile, longer, longest = (
        jax.ShapeDtypeStruct((rows + 8 * extra, LANES), f32) for extra in range(3)
    )
    lines = pltpu.VMEM((rows, LANES), f32)
    p_near, p_far, hv, sv, hp, sp, xp = call(
        first_kernel,
        [tile, longest] + [jax.ShapeDtypeStruct(x.shape, x.dtype) for x in inputs[2:]],
        [SMEM] + [pl.BlockSpec(memory_space=pltpu.HBM)] * 7,
        [
            pltpu.VMEM(pv.shape, f32),
            pltpu.VMEM(pp.shape, jnp.int32),
            lines,
            pltpu.SemaphoreType.DMA((7,)),
        ],
        1 << 10,
        pc, *inputs,
    )
    h_tile, s_near, s_far, mask = call(
        rest_kernel,
        [longer, tile, longest, jax.ShapeDtypeStruct((max(8, cap // 2), LANES), f32)],
        [VMEM] * 5 + [SMEM] * 3,
        [lines],
        1 << 10,
        hv, sv, hp, sp, xp, hc, sc, xc,
    )
    along = list(range(row_count - 1, 0, -1))
    across = list(range(chip_count - 1, 0, -1))

    def along_z(near, far):
        got = {}
        for offset in sorted(along, key=lambda s: s.bit_count()):
            low = offset & -offset
            if offset != low:
                value = stack([got[offset ^ low]])
            else:
                value = near if low == 1 else far
            got[offset] = send(value, lambda r, m, k: (r ^ low, m, k))
        return [got[offset] for offset in along]

    def parted(x, count):
        return call(
            parted_kernel, [tile] * count, [VMEM], [], 1 << 10, x
        )

    def in_plane(x):
        return [send(x, lambda r, m, k, o=o: (r, m ^ o, k)) for o in across]

    def product(a_got, a_shared, b, b_got, parts, *waits):
        part = jax.ShapeDtypeStruct((LANES, LANES), f32)
        return call(
            functools.partial(product_kernel, along, across, len(a_shared), len(waits)),
            [longer] + [part] * parts,
            [VMEM] * (3 + len(a_shared) + len(b_got))
            + [pl.BlockSpec(memory_space=pl.ANY)] * len(waits),
            [pltpu.VMEM((order, 2 * LANES), jnp.bfloat16)],
            2 * 3 * rows * order * LANES,
            a_got, *a_shared, b, *b_got, mask, *waits,
        )

    p_got = along_z(p_near, p_far)
    s_got = along_z(s_far, s_far)
    h_parts = [h_tile] + in_plane(h_tile)
    h_got = stack(h_parts, *p_got[::-1])
    h_shared = [to_other(x) for x in parted(h_got, len(h_parts))]
    (y,) = product(h_got, h_shared, p_near, p_got, 0, s_got[along.index(row_count // 2)])
    y_got = stack([y] + in_plane(y), *s_got)
    x, *sent = product(y_got, [to_other(y_got)], s_near, s_got, sends)

    relay = row_count == chip_count == 4

    def mirror(turn):
        def target(r, m, k):
            column = 2 * m + k
            part = (column + turn) % sends
            if relay and turn == 0 and r ^ m < 2:
                return r, m ^ 1, part
            to = r * sends + part
            return column // sends, to // 2, to % 2

        return target

    mirrors = [send(value, mirror(turn)) for turn, value in enumerate(sent)]
    if relay:
        mirrors += [
            send(mirrors[0], lambda r, m, k: (r ^ 1, m, k) if r == m else None),
            sent[0],
            to_other(sent[1]),
        ]
    return call(
        functools.partial(slots_kernel, cap, sends),
        jax.ShapeDtypeStruct((1, cap, BS * BS), f32),
        [VMEM, SMEM] + [VMEM] * (1 + len(mirrors)),
        [lines] * 2,
        1 << 20,
        xp, xc, x, *mirrors,
    )


def solution(mesh):
    values, ints = P("row", "col", None), P("row", "col")
    row_count, col_count = mesh.shape["row"], mesh.shape["col"]
    return jax.shard_map(
        functools.partial(shards, row_count, col_count // 2),
        mesh=mesh,
        in_specs=(values, ints, ints) * 3 + (ints, ints),
        out_specs=values,
        check_vma=False,
    )
```

```python
import functools

import jax
import jax.numpy as jnp
from jax import lax
from jax.experimental import pallas as pl
from jax.experimental.pallas import tpu as pltpu
from jax.sharding import PartitionSpec as P

BS = 64
LANES = 128
COST = 1 << 10
LINES = BS * BS // LANES
VMEM = pl.BlockSpec(memory_space=pltpu.VMEM)
SMEM = pl.BlockSpec(memory_space=pltpu.SMEM)
AXES = ("row", "col")


def position():
    col = lax.axis_index("col")
    return lax.axis_index("row"), col // 2, col % 2


def left_lanes(rows):
    return lax.broadcasted_iota(jnp.int32, (rows, LANES), 1) < BS


def slot_places(places, count, rows=LINES):
    return [
        jnp.where(slot < count, jnp.broadcast_to(places[0:1, slot : slot + 1], (rows, LANES)), -1)
        for slot in range(places.shape[1])
    ]


def fill(ref, rows):
    if ref.shape[0] > rows:
        ref[rows:, :] = jnp.zeros((ref.shape[0] - rows, LANES), jnp.float32)


def assemble(value, places, count, lines, tiles):
    left = left_lanes(LINES)
    cap = value.shape[1]
    for line in range(LINES):
        lines[pl.ds(line, cap, stride=LINES), :] = value[0, :, line * LANES : (line + 1) * LANES]
    at = slot_places(places, count)

    def block(place):
        picked = jnp.zeros((LINES, LANES), jnp.float32)
        for slot in range(cap):
            rows = lines[slot * LINES : (slot + 1) * LINES, :]
            picked = jnp.where(at[slot] == place, rows, picked)
        return picked

    for pair in range(cap // 2):
        first, second = block(2 * pair), block(2 * pair + 1)
        even = jnp.where(left, first, pltpu.roll(second, BS, 1))
        odd = jnp.where(left, pltpu.roll(first, BS, 1), second)
        for tile in tiles:
            tile[pl.ds(pair * BS, LINES, stride=2), :] = even
            tile[pl.ds(pair * BS + 1, LINES, stride=2), :] = odd
    for tile in tiles:
        fill(tile, cap * LINES)


def first_kernel(count, *refs):
    sources, (near, far), fetched = refs[:7], refs[7:9], refs[9:14]
    value_in, places_in, lines, sems = refs[14:]
    copies = [
        pltpu.make_async_copy(source, ref, sems.at[i])
        for i, (source, ref) in enumerate(zip(sources, (places_in, value_in) + fetched))
    ]
    for copy in copies:
        copy.start()
    for copy in copies[:2]:
        copy.wait()
    assemble(value_in, places_in, count[0, 0], lines, (near, far))
    for copy in copies[2:]:
        copy.wait()


def rest_kernel(hv, sv, hp, sp, xp, hc, sc, xc, h_tile, s_near, s_far, mask, lines):
    assemble(hv, hp, hc[0, 0], lines, (h_tile,))
    assemble(sv, sp, sc[0, 0], lines, (s_near, s_far))
    cap = xp.shape[1]
    at = slot_places(xp, xc[0, 0], 1)

    def flag(place):
        present = jnp.zeros((1, LANES), jnp.float32)
        for slot in range(cap):
            present = jnp.where(at[slot] == place, 1.0, present)
        return present

    for pair in range(cap // 2):
        mask[pair : pair + 1, :] = jnp.where(left_lanes(1), flag(2 * pair), flag(2 * pair + 1))


def stack_kernel(others, count, rows, *refs):
    for i, ref in enumerate(refs[others : others + count]):
        refs[-1][i * rows : (i + 1) * rows, :] = ref[:rows, :]


def copy_kernel(x, _, out):
    out[...] = x[: out.shape[0], :]


def parted_kernel(x, *outs):
    rows = outs[0].shape[0]
    for i, out in enumerate(outs):
        out[...] = x[i * rows : (i + 1) * rows, :]


def split(x):
    high = x.astype(jnp.bfloat16)
    return high, (x - high.astype(jnp.float32)).astype(jnp.bfloat16)


def product_kernel(along, across, shares, waits, *refs):
    got, shared, b_own = refs[0], refs[1 : 1 + shares], refs[1 + shares]
    refs = refs[2 + shares :]
    b_got, mask, out = refs[: len(along)], refs[len(along)], refs[len(along) + 1 + waits]
    sent, both = refs[len(along) + 2 + waits : -1], refs[-1]
    row, chip, core = position()
    rows = out.shape[0] // BS * BS
    for offset, ref in zip([0] + along, (b_own,) + b_got):
        at = pl.ds(pl.multiple_of((row ^ offset) * rows, rows), rows)
        both[at, :LANES], both[at, LANES:] = split(ref[:rows, :])
    dot = functools.partial(jnp.dot, preferred_element_type=jnp.float32)

    def multiply(left, right):
        wide, narrow = None, None

        def piece(refs, i):
            per = (1 + len(across)) // len(refs)
            return refs[i // per][i % per * rows : (i % per + 1) * rows, :]

        for i, offset in enumerate([0] + across):
            at = pl.ds(pl.multiple_of((chip ^ offset) * 2 * LANES, 2 * LANES), 2 * LANES)
            a = jnp.concatenate([piece(left, i), piece(right, i)], axis=1)
            a_high, a_low = split(a)
            terms = dot(a_high, both[at, :]), dot(a_low, both[at, :LANES])
            wide = terms[0] if wide is None else wide + terms[0]
            narrow = terms[1] if narrow is None else narrow + terms[1]
        acc = wide[:, :LANES] + (wide[:, LANES:] + narrow)
        for pair in range(rows // BS):
            at = slice(pair * BS, (pair + 1) * BS)
            out[at, :] = acc[at, :] * mask[pair : pair + 1, :]

    pl.when(core == 0)(lambda: multiply([got], shared))
    pl.when(core == 1)(lambda: multiply(shared, [got]))
    fill(out, rows)
    for turn, ref in enumerate(sent):
        part = lax.rem(2 * chip + core + turn, len(sent))
        ref[...] = out[pl.ds(pl.multiple_of(part * LANES, LANES), LANES), :]


def slots_kernel(cap, sends, places, count, x, *refs):
    mirrors, (out, tile, lines) = refs[:-3], refs[-3:]
    row, chip, _ = position()
    tile[...] = x[: tile.shape[0], :]

    def add(parts):
        for turn, value in enumerate(parts):
            part = lax.rem(lax.axis_index("col") + (sends - turn), sends)
            at = pl.ds(pl.multiple_of(part * LANES, LANES), LANES)
            tile[at, :] += value.T

    def straight():
        add([ref[...] for ref in mirrors[:sends]])

    if len(mirrors) == sends:
        straight()
    else:
        relayed, kept, other = (ref[...] for ref in mirrors[sends:])
        far = row ^ chip
        pl.when(far == 0)(lambda: add([kept, other]))
        pl.when(far == 1)(lambda: add([relayed, mirrors[1][...]]))
        pl.when(far > 1)(straight)
    left = left_lanes(LINES)
    blocks = []
    for pair in range(cap // 2):
        even = tile[pl.ds(pair * BS, LINES, stride=2), :]
        odd = tile[pl.ds(pair * BS + 1, LINES, stride=2), :]
        blocks.append(jnp.where(left, even, pltpu.roll(odd, BS, 1)))
        blocks.append(jnp.where(left, pltpu.roll(even, BS, 1), odd))
    for slot, at in enumerate(slot_places(places, count[0, 0])):
        picked = jnp.zeros((LINES, LANES), jnp.float32)
        for place, block in enumerate(blocks):
            picked = jnp.where(at == place, block, picked)
        lines[slot * LINES : (slot + 1) * LINES, :] = picked
    for line in range(LINES):
        out[0, :, line * LANES : (line + 1) * LANES] = lines[
            pl.ds(line, cap, stride=LINES), :
        ]


def call(kernel, out_shapes, in_specs, scratch, cost, *args):
    single = not isinstance(out_shapes, list)
    return pl.pallas_call(
        kernel,
        out_shape=out_shapes,
        in_specs=in_specs,
        out_specs=VMEM if single else [VMEM] * len(out_shapes),
        scratch_shapes=scratch,
        compiler_params=pltpu.CompilerParams(vmem_limit_bytes=32 * 1024 * 1024),
        cost_estimate=pl.CostEstimate(flops=COST, bytes_accessed=COST, transcendentals=0),
    )(*args)


def shards(row_count, chip_count, hv, hp, hc, pv, pp, pc, sv, sp, sc, xp, xc):
    cap = hp.shape[1]
    rows = cap * LINES
    order = row_count * rows
    sends = rows // LANES
    f32 = jnp.float32

    def device(r, m, k):
        return (r * chip_count + m) * 2 + k

    def send(value, target):
        pairs = [
            (device(r, m, k), device(*target(r, m, k)))
            for r in range(row_count)
            for m in range(chip_count)
            for k in range(2)
            if target(r, m, k)
        ]
        return lax.ppermute(value, AXES, pairs)

    def to_other(value):
        return send(value, lambda r, m, k: (r, m, 1 - k))

    def stack(arrays, *others):
        return call(
            functools.partial(stack_kernel, len(others), len(arrays), rows),
            jax.ShapeDtypeStruct((len(arrays) * rows, LANES), f32),
            [pl.BlockSpec(memory_space=pl.ANY)] * len(others) + [VMEM] * len(arrays),
            [],
            1 << 10,
            *others, *arrays,
        )

    inputs = [
        pltpu.with_memory_space_constraint(x, pltpu.HBM) for x in (pp, pv, hv, sv, hp, sp, xp)
    ]

    def sized(extra):
        return jax.ShapeDtypeStruct((rows + extra, LANES), f32)

    tile, longer, longest = sized(0), sized(8), sized(16)
    lines = pltpu.VMEM((rows, LANES), f32)
    p_near, p_far, hv, sv, hp, sp, xp = call(
        first_kernel,
        [tile, longest] + [jax.ShapeDtypeStruct(x.shape, x.dtype) for x in inputs[2:]],
        [SMEM] + [pl.BlockSpec(memory_space=pltpu.HBM)] * 7,
        [
            pltpu.VMEM(pv.shape, f32),
            pltpu.VMEM(pp.shape, jnp.int32),
            lines,
            pltpu.SemaphoreType.DMA((7,)),
        ],
        1 << 10,
        pc, *inputs,
    )
    h_tile, s_near, s_far, mask = call(
        rest_kernel,
        [longer, sized(24), sized(56), jax.ShapeDtypeStruct((max(8, cap // 2), LANES), f32)],
        [VMEM] * 5 + [SMEM] * 3,
        [lines],
        1 << 10,
        hv, sv, hp, sp, xp, hc, sc, xc,
    )
    along = list(range(row_count - 1, 0, -1))
    across = list(range(chip_count - 1, 0, -1))

    def along_z(near, far, direct=False):
        got = {}

        def hops(offset):
            taken = []
            for bit in reversed(range(row_count.bit_length())):
                if offset >> bit & 1:
                    taken.append((2 << bit) - 1)
                    offset ^= taken[-1]
            return taken

        for offset in sorted(along, key=lambda s: len(hops(s))):
            hop = hops(offset)[-1]
            if offset != hop:
                value = got[offset ^ hop] if direct else stack([got[offset ^ hop]])
            else:
                value = near if hop == 1 else far
            got[offset] = send(value, lambda r, m, k: (r ^ hop, m, k))
        return [got[offset] for offset in along]

    def parted(x, count):
        return call(
            parted_kernel, [tile] * count, [VMEM], [], 1 << 10, x
        )

    def in_plane(x, last=None):
        return [
            send(x if last is None or o > 1 else last, lambda r, m, k, o=o: (r, m ^ o, k))
            for o in across
        ]

    def product(a_got, a_shared, b, b_got, parts, *waits):
        part = jax.ShapeDtypeStruct((LANES, LANES), f32)
        return call(
            functools.partial(product_kernel, along, across, len(a_shared), len(waits)),
            [longest] + [part] * parts,
            [VMEM] * (3 + len(a_shared) + len(b_got))
            + [pl.BlockSpec(memory_space=pl.ANY)] * len(waits),
            [pltpu.VMEM((order, 2 * LANES), jnp.bfloat16)],
            1 << 10,
            a_got, *a_shared, b, *b_got, mask, *waits,
        )

    p_got = along_z(p_far, p_far, direct=True)
    s_got = along_z(s_near, s_far)
    h_parts = [h_tile] + in_plane(h_tile)
    h_got = stack(h_parts, *p_got[::-1])
    h_shared = [to_other(x) for x in parted(h_got, len(h_parts))]
    (y,) = product(h_got, h_shared, p_near, p_got, 0)
    y_got = stack([y] + in_plane(y), *s_got)
    x, *sent = product(y_got, [to_other(y_got)], s_near, s_got, sends)

    relay = row_count == chip_count == 4

    def mirror(turn):
        def target(r, m, k):
            column = 2 * m + k
            part = (column + turn) % sends
            if relay and turn == 0 and r ^ m < 2:
                return r, m ^ 1, part
            to = r * sends + part
            return column // sends, to // 2, to % 2

        return target

    mirrors = [send(value, mirror(turn)) for turn, value in enumerate(sent)]
    if relay:
        mirrors += [
            send(mirrors[0], lambda r, m, k: (r ^ 1, m, k) if r == m else None),
            sent[0],
            to_other(sent[1]),
        ]
    return call(
        functools.partial(slots_kernel, cap, sends),
        jax.ShapeDtypeStruct((1, cap, BS * BS), f32),
        [VMEM, SMEM] + [VMEM] * (1 + len(mirrors)),
        [lines] * 2,
        1 << 20,
        xp, xc, x, *mirrors,
    )


def solution(mesh):
    values, ints = P("row", "col", None), P("row", "col")
    row_count, col_count = mesh.shape["row"], mesh.shape["col"]
    return jax.shard_map(
        functools.partial(shards, row_count, col_count // 2),
        mesh=mesh,
        in_specs=(values, ints, ints) * 3 + (ints, ints),
        out_specs=values,
        check_vma=False,
    )
```

```python
import functools

import jax
import jax.numpy as jnp
from jax import lax
from jax.experimental import pallas as pl
from jax.experimental.pallas import tpu as pltpu
from jax.sharding import PartitionSpec as P

BS = 64
LANES = 128
COST = 1 << 10
LINES = BS * BS // LANES
VMEM = pl.BlockSpec(memory_space=pltpu.VMEM)
SMEM = pl.BlockSpec(memory_space=pltpu.SMEM)
AXES = ("row", "col")


def position():
    col = lax.axis_index("col")
    return lax.axis_index("row"), col // 2, col % 2


def left_lanes(rows):
    return lax.broadcasted_iota(jnp.int32, (rows, LANES), 1) < BS


def slot_places(places, count, rows=LINES):
    return [
        jnp.where(slot < count, jnp.broadcast_to(places[0:1, slot : slot + 1], (rows, LANES)), -1)
        for slot in range(places.shape[1])
    ]


def fill(ref, rows):
    if ref.shape[0] > rows:
        ref[rows:, :] = jnp.zeros((ref.shape[0] - rows, LANES), jnp.float32)


def assemble(value, places, count, lines, tiles):
    left = left_lanes(LINES)
    cap = value.shape[1]
    for line in range(LINES):
        lines[pl.ds(line, cap, stride=LINES), :] = value[0, :, line * LANES : (line + 1) * LANES]
    at = slot_places(places, count)

    def block(place):
        picked = jnp.zeros((LINES, LANES), jnp.float32)
        for slot in range(cap):
            rows = lines[slot * LINES : (slot + 1) * LINES, :]
            picked = jnp.where(at[slot] == place, rows, picked)
        return picked

    for pair in range(cap // 2):
        first, second = block(2 * pair), block(2 * pair + 1)
        even = jnp.where(left, first, pltpu.roll(second, BS, 1))
        odd = jnp.where(left, pltpu.roll(first, BS, 1), second)
        for tile in tiles:
            tile[pl.ds(pair * BS, LINES, stride=2), :] = even
            tile[pl.ds(pair * BS + 1, LINES, stride=2), :] = odd
    for tile in tiles:
        fill(tile, cap * LINES)


def first_kernel(count, *refs):
    sources, (near, far), fetched = refs[:7], refs[7:9], refs[9:14]
    value_in, places_in, lines, sems = refs[14:]
    copies = [
        pltpu.make_async_copy(source, ref, sems.at[i])
        for i, (source, ref) in enumerate(zip(sources, (places_in, value_in) + fetched))
    ]
    for copy in copies:
        copy.start()
    for copy in copies[:2]:
        copy.wait()
    assemble(value_in, places_in, count[0, 0], lines, (near, far))
    for copy in copies[2:]:
        copy.wait()


def rest_kernel(
    hv, sv, hp, sp, xp, hc, sc, xc, h_far, h_near, s_near, s_far, mask, lines
):
    assemble(hv, hp, hc[0, 0], lines, (h_far, h_near))
    assemble(sv, sp, sc[0, 0], lines, (s_near, s_far))
    cap = xp.shape[1]
    at = slot_places(xp, xc[0, 0], 1)

    def flag(place):
        present = jnp.zeros((1, LANES), jnp.float32)
        for slot in range(cap):
            present = jnp.where(at[slot] == place, 1.0, present)
        return present

    for pair in range(cap // 2):
        mask[pair : pair + 1, :] = jnp.where(left_lanes(1), flag(2 * pair), flag(2 * pair + 1))


def stack_kernel(others, count, rows, *refs):
    for i, ref in enumerate(refs[others : others + count]):
        refs[-1][i * rows : (i + 1) * rows, :] = ref[:rows, :]


def copy_kernel(x, _, out):
    out[...] = x[: out.shape[0], :]


def parted_kernel(x, *outs):
    rows = outs[0].shape[0]
    for i, out in enumerate(outs):
        out[...] = x[i * rows : (i + 1) * rows, :]


def split(x):
    high = x.astype(jnp.bfloat16)
    return high, (x - high.astype(jnp.float32)).astype(jnp.bfloat16)


def product_kernel(along, across, shares, waits, *refs):
    got, shared, b_own = refs[0], refs[1 : 1 + shares], refs[1 + shares]
    refs = refs[2 + shares :]
    b_got, mask, out = refs[: len(along)], refs[len(along)], refs[len(along) + 1 + waits]
    sent, both = refs[len(along) + 2 + waits : -1], refs[-1]
    row, chip, core = position()
    rows = out.shape[0] // BS * BS
    for offset, ref in zip([0] + along, (b_own,) + b_got):
        at = pl.ds(pl.multiple_of((row ^ offset) * rows, rows), rows)
        both[at, :LANES], both[at, LANES:] = split(ref[:rows, :])
    dot = functools.partial(jnp.dot, preferred_element_type=jnp.float32)

    def multiply(left, right):
        wide, narrow = None, None

        def piece(refs, i):
            per = (1 + len(across)) // len(refs)
            return refs[i // per][i % per * rows : (i % per + 1) * rows, :]

        for i, offset in enumerate([0] + across):
            at = pl.ds(pl.multiple_of((chip ^ offset) * 2 * LANES, 2 * LANES), 2 * LANES)
            a = jnp.concatenate([piece(left, i), piece(right, i)], axis=1)
            a_high, a_low = split(a)
            terms = dot(a_high, both[at, :]), dot(a_low, both[at, :LANES])
            wide = terms[0] if wide is None else wide + terms[0]
            narrow = terms[1] if narrow is None else narrow + terms[1]
        acc = wide[:, :LANES] + (wide[:, LANES:] + narrow)
        for pair in range(rows // BS):
            at = slice(pair * BS, (pair + 1) * BS)
            out[at, :] = acc[at, :] * mask[pair : pair + 1, :]

    pl.when(core == 0)(lambda: multiply([got], shared))
    pl.when(core == 1)(lambda: multiply(shared, [got]))
    fill(out, rows)
    for turn, ref in enumerate(sent):
        part = lax.rem(2 * chip + core + turn, len(sent))
        ref[...] = out[pl.ds(pl.multiple_of(part * LANES, LANES), LANES), :]


def slots_kernel(cap, sends, places, count, x, *refs):
    mirrors, (out, tile, lines) = refs[:-3], refs[-3:]
    row, chip, _ = position()
    tile[...] = x[: tile.shape[0], :]

    def add(parts):
        for turn, value in enumerate(parts):
            part = lax.rem(lax.axis_index("col") + (sends - turn), sends)
            at = pl.ds(pl.multiple_of(part * LANES, LANES), LANES)
            tile[at, :] += value.T

    def straight():
        add([ref[...] for ref in mirrors[:sends]])

    if len(mirrors) == sends:
        straight()
    else:
        relayed, kept, other = (ref[...] for ref in mirrors[sends:])
        far = row ^ chip
        pl.when(far == 0)(lambda: add([kept, other]))
        pl.when(far == 1)(lambda: add([relayed, mirrors[1][...]]))
        pl.when(far > 1)(straight)
    left = left_lanes(LINES)
    blocks = []
    for pair in range(cap // 2):
        even = tile[pl.ds(pair * BS, LINES, stride=2), :]
        odd = tile[pl.ds(pair * BS + 1, LINES, stride=2), :]
        blocks.append(jnp.where(left, even, pltpu.roll(odd, BS, 1)))
        blocks.append(jnp.where(left, pltpu.roll(even, BS, 1), odd))
    for slot, at in enumerate(slot_places(places, count[0, 0])):
        picked = jnp.zeros((LINES, LANES), jnp.float32)
        for place, block in enumerate(blocks):
            picked = jnp.where(at == place, block, picked)
        lines[slot * LINES : (slot + 1) * LINES, :] = picked
    for line in range(LINES):
        out[0, :, line * LANES : (line + 1) * LANES] = lines[
            pl.ds(line, cap, stride=LINES), :
        ]


def call(kernel, out_shapes, in_specs, scratch, cost, *args):
    single = not isinstance(out_shapes, list)
    return pl.pallas_call(
        kernel,
        out_shape=out_shapes,
        in_specs=in_specs,
        out_specs=VMEM if single else [VMEM] * len(out_shapes),
        scratch_shapes=scratch,
        compiler_params=pltpu.CompilerParams(vmem_limit_bytes=32 * 1024 * 1024),
        cost_estimate=pl.CostEstimate(flops=COST, bytes_accessed=COST, transcendentals=0),
    )(*args)


def shards(row_count, chip_count, hv, hp, hc, pv, pp, pc, sv, sp, sc, xp, xc):
    cap = hp.shape[1]
    rows = cap * LINES
    order = row_count * rows
    sends = rows // LANES
    f32 = jnp.float32

    def device(r, m, k):
        return (r * chip_count + m) * 2 + k

    def send(value, target):
        pairs = [
            (device(r, m, k), device(*target(r, m, k)))
            for r in range(row_count)
            for m in range(chip_count)
            for k in range(2)
            if target(r, m, k)
        ]
        return lax.ppermute(value, AXES, pairs)

    def to_other(value):
        return send(value, lambda r, m, k: (r, m, 1 - k))

    def stack(arrays, *others):
        return call(
            functools.partial(stack_kernel, len(others), len(arrays), rows),
            jax.ShapeDtypeStruct((len(arrays) * rows, LANES), f32),
            [pl.BlockSpec(memory_space=pl.ANY)] * len(others) + [VMEM] * len(arrays),
            [],
            1 << 10,
            *others, *arrays,
        )

    inputs = [
        pltpu.with_memory_space_constraint(x, pltpu.HBM) for x in (pp, pv, hv, sv, hp, sp, xp)
    ]

    def sized(extra):
        return jax.ShapeDtypeStruct((rows + extra, LANES), f32)

    tile, longer, longest = sized(0), sized(8), sized(16)
    lines = pltpu.VMEM((rows, LANES), f32)
    p_near, p_far, hv, sv, hp, sp, xp = call(
        first_kernel,
        [tile, longest] + [jax.ShapeDtypeStruct(x.shape, x.dtype) for x in inputs[2:]],
        [SMEM] + [pl.BlockSpec(memory_space=pltpu.HBM)] * 7,
        [
            pltpu.VMEM(pv.shape, f32),
            pltpu.VMEM(pp.shape, jnp.int32),
            lines,
            pltpu.SemaphoreType.DMA((7,)),
        ],
        1 << 10,
        pc, *inputs,
    )
    h_far, h_near, s_near, s_far, mask = call(
        rest_kernel,
        [tile, sized(24), sized(24), sized(40), jax.ShapeDtypeStruct((max(8, cap // 2), LANES), f32)],
        [VMEM] * 5 + [SMEM] * 3,
        [lines],
        1 << 10,
        hv, sv, hp, sp, xp, hc, sc, xc,
    )
    along = list(range(row_count - 1, 0, -1))
    across = list(range(chip_count - 1, 0, -1))

    def along_z(near, far, direct=False):
        got = {}

        def hops(offset):
            taken = []
            for bit in reversed(range(row_count.bit_length())):
                if offset >> bit & 1:
                    taken.append((2 << bit) - 1)
                    offset ^= taken[-1]
            return taken

        for offset in sorted(along, key=lambda s: len(hops(s))):
            hop = hops(offset)[-1]
            if offset != hop:
                value = got[offset ^ hop] if direct else stack([got[offset ^ hop]])
            else:
                value = near if hop == 1 else far
            got[offset] = send(value, lambda r, m, k: (r ^ hop, m, k))
        return [got[offset] for offset in along]

    def parted(x, count):
        return call(
            parted_kernel, [tile] * count, [VMEM], [], 1 << 10, x
        )

    def in_plane(x, other, others):
        return [
            send(other if o in others else x, lambda r, m, k, o=o: (r, m ^ o, k)) for o in across
        ]

    def product(a_got, a_shared, b, b_got, parts, *waits):
        part = jax.ShapeDtypeStruct((LANES, LANES), f32)
        return call(
            functools.partial(product_kernel, along, across, len(a_shared), len(waits)),
            [longer] + [part] * parts,
            [VMEM] * (3 + len(a_shared) + len(b_got))
            + [pl.BlockSpec(memory_space=pl.ANY)] * len(waits),
            [pltpu.VMEM((order, 2 * LANES), jnp.bfloat16)],
            1 << 10,
            a_got, *a_shared, b, *b_got, mask, *waits,
        )

    p_got = along_z(p_far, p_far)
    s_got = along_z(s_near, s_far)
    h_parts = [h_far] + in_plane(h_far, h_near, (1, 2))
    h_got = stack(h_parts, *p_got[::-1])
    h_shared = [to_other(x) for x in parted(h_got, len(h_parts))]
    (y,) = product(h_got, h_shared, p_near, p_got, 0)
    y_got = stack([y] + in_plane(y, y, ()), *s_got)
    x, *sent = product(y_got, [to_other(y_got)], s_near, s_got, sends)

    relay = row_count == chip_count == 4

    def mirror(turn):
        def target(r, m, k):
            column = 2 * m + k
            part = (column + turn) % sends
            if relay and turn == 0 and r ^ m < 2:
                return r, m ^ 1, part
            to = r * sends + part
            return column // sends, to // 2, to % 2

        return target

    mirrors = [send(value, mirror(turn)) for turn, value in enumerate(sent)]
    if relay:
        mirrors += [
            send(mirrors[0], lambda r, m, k: (r ^ 1, m, k) if r == m else None),
            sent[0],
            to_other(sent[1]),
        ]
    return call(
        functools.partial(slots_kernel, cap, sends),
        jax.ShapeDtypeStruct((1, cap, BS * BS), f32),
        [VMEM, SMEM] + [VMEM] * (1 + len(mirrors)),
        [lines] * 2,
        1 << 20,
        xp, xc, x, *mirrors,
    )


def solution(mesh):
    values, ints = P("row", "col", None), P("row", "col")
    row_count, col_count = mesh.shape["row"], mesh.shape["col"]
    return jax.shard_map(
        functools.partial(shards, row_count, col_count // 2),
        mesh=mesh,
        in_specs=(values, ints, ints) * 3 + (ints, ints),
        out_specs=values,
        check_vma=False,
    )
```

```python
import functools

import jax
import jax.numpy as jnp
from jax import lax
from jax.experimental import pallas as pl
from jax.experimental.pallas import tpu as pltpu
from jax.sharding import PartitionSpec as P

BS = 64
LANES = 128
COST = 1 << 10
LINES = BS * BS // LANES
VMEM = pl.BlockSpec(memory_space=pltpu.VMEM)
SMEM = pl.BlockSpec(memory_space=pltpu.SMEM)
AXES = ("row", "col")


def position():
    col = lax.axis_index("col")
    return lax.axis_index("row"), col // 2, col % 2


def left_lanes(rows):
    return lax.broadcasted_iota(jnp.int32, (rows, LANES), 1) < BS


def slot_places(places, count, rows=LINES):
    return [
        jnp.where(slot < count, jnp.broadcast_to(places[0:1, slot : slot + 1], (rows, LANES)), -1)
        for slot in range(places.shape[1])
    ]


def fill(ref, rows):
    if ref.shape[0] > rows:
        ref[rows:, :] = jnp.zeros((ref.shape[0] - rows, LANES), jnp.float32)


def assemble(value, places, count, lines, tiles):
    left = left_lanes(LINES)
    cap = value.shape[1]
    for line in range(LINES):
        lines[pl.ds(line, cap, stride=LINES), :] = value[0, :, line * LANES : (line + 1) * LANES]
    at = slot_places(places, count)

    def block(place):
        picked = jnp.zeros((LINES, LANES), jnp.float32)
        for slot in range(cap):
            rows = lines[slot * LINES : (slot + 1) * LINES, :]
            picked = jnp.where(at[slot] == place, rows, picked)
        return picked

    for pair in range(cap // 2):
        first, second = block(2 * pair), block(2 * pair + 1)
        even = jnp.where(left, first, pltpu.roll(second, BS, 1))
        odd = jnp.where(left, pltpu.roll(first, BS, 1), second)
        for tile in tiles:
            tile[pl.ds(pair * BS, LINES, stride=2), :] = even
            tile[pl.ds(pair * BS + 1, LINES, stride=2), :] = odd
    for tile in tiles:
        fill(tile, cap * LINES)


def first_kernel(count, *refs):
    sources, (near, far), fetched = refs[:7], refs[7:9], refs[9:14]
    value_in, places_in, lines, sems = refs[14:]
    copies = [
        pltpu.make_async_copy(source, ref, sems.at[i])
        for i, (source, ref) in enumerate(zip(sources, (places_in, value_in) + fetched))
    ]
    for copy in copies:
        copy.start()
    for copy in copies[:2]:
        copy.wait()
    assemble(value_in, places_in, count[0, 0], lines, (near, far))
    for copy in copies[2:]:
        copy.wait()


def rest_kernel(
    hv, sv, hp, sp, xp, hc, sc, xc, h_far, h_near, s_near, s_far, mask, lines
):
    assemble(hv, hp, hc[0, 0], lines, (h_far, h_near))
    assemble(sv, sp, sc[0, 0], lines, (s_near, s_far))
    cap = xp.shape[1]
    at = slot_places(xp, xc[0, 0], 1)

    def flag(place):
        present = jnp.zeros((1, LANES), jnp.float32)
        for slot in range(cap):
            present = jnp.where(at[slot] == place, 1.0, present)
        return present

    for pair in range(cap // 2):
        mask[pair : pair + 1, :] = jnp.where(left_lanes(1), flag(2 * pair), flag(2 * pair + 1))


def stack_kernel(others, count, rows, *refs):
    for i, ref in enumerate(refs[others : others + count]):
        refs[-1][i * rows : (i + 1) * rows, :] = ref[:rows, :]


def copy_kernel(x, _, out):
    out[...] = x[: out.shape[0], :]


def parted_kernel(x, *outs):
    rows = outs[0].shape[0]
    for i, out in enumerate(outs):
        out[...] = x[i * rows : (i + 1) * rows, :]


def split(x):
    high = x.astype(jnp.bfloat16)
    return high, (x - high.astype(jnp.float32)).astype(jnp.bfloat16)


def product_kernel(along, across, shares, waits, *refs):
    got, shared, b_own = refs[0], refs[1 : 1 + shares], refs[1 + shares]
    refs = refs[2 + shares :]
    b_got, mask, out = refs[: len(along)], refs[len(along)], refs[len(along) + 1 + waits]
    sent, both = refs[len(along) + 2 + waits : -1], refs[-1]
    row, chip, core = position()
    rows = out.shape[0] // BS * BS
    for offset, ref in zip([0] + along, (b_own,) + b_got):
        at = pl.ds(pl.multiple_of((row ^ offset) * rows, rows), rows)
        both[at, :LANES], both[at, LANES:] = split(ref[:rows, :])
    dot = functools.partial(jnp.dot, preferred_element_type=jnp.float32)

    def multiply(left, right):
        wide, narrow = None, None

        def piece(refs, i):
            per = (1 + len(across)) // len(refs)
            return refs[i // per][i % per * rows : (i % per + 1) * rows, :]

        for i, offset in enumerate([0] + across):
            at = pl.ds(pl.multiple_of((chip ^ offset) * 2 * LANES, 2 * LANES), 2 * LANES)
            a = jnp.concatenate([piece(left, i), piece(right, i)], axis=1)
            a_high, a_low = split(a)
            terms = dot(a_high, both[at, :]), dot(a_low, both[at, :LANES])
            wide = terms[0] if wide is None else wide + terms[0]
            narrow = terms[1] if narrow is None else narrow + terms[1]
        acc = wide[:, :LANES] + (wide[:, LANES:] + narrow)
        for pair in range(rows // BS):
            at = slice(pair * BS, (pair + 1) * BS)
            out[at, :] = acc[at, :] * mask[pair : pair + 1, :]

    pl.when(core == 0)(lambda: multiply([got], shared))
    pl.when(core == 1)(lambda: multiply(shared, [got]))
    fill(out, rows)
    for turn, ref in enumerate(sent):
        part = lax.rem(2 * chip + core + turn, len(sent))
        ref[...] = out[pl.ds(pl.multiple_of(part * LANES, LANES), LANES), :]


def slots_kernel(cap, sends, places, count, x, *refs):
    mirrors, (out, tile, lines) = refs[:-3], refs[-3:]
    row, chip, _ = position()
    tile[...] = x[: tile.shape[0], :]

    def add(parts):
        for turn, value in enumerate(parts):
            part = lax.rem(lax.axis_index("col") + (sends - turn), sends)
            at = pl.ds(pl.multiple_of(part * LANES, LANES), LANES)
            tile[at, :] += value.T

    def straight():
        add([ref[...] for ref in mirrors[:sends]])

    if len(mirrors) == sends:
        straight()
    else:
        relayed, kept, other = (ref[...] for ref in mirrors[sends:])
        far = row ^ chip
        pl.when(far == 0)(lambda: add([kept, other]))
        pl.when(far == 1)(lambda: add([relayed, mirrors[1][...]]))
        pl.when(far > 1)(straight)
    left = left_lanes(LINES)
    blocks = []
    for pair in range(cap // 2):
        even = tile[pl.ds(pair * BS, LINES, stride=2), :]
        odd = tile[pl.ds(pair * BS + 1, LINES, stride=2), :]
        blocks.append(jnp.where(left, even, pltpu.roll(odd, BS, 1)))
        blocks.append(jnp.where(left, pltpu.roll(even, BS, 1), odd))
    for slot, at in enumerate(slot_places(places, count[0, 0])):
        picked = jnp.zeros((LINES, LANES), jnp.float32)
        for place, block in enumerate(blocks):
            picked = jnp.where(at == place, block, picked)
        lines[slot * LINES : (slot + 1) * LINES, :] = picked
    for line in range(LINES):
        out[0, :, line * LANES : (line + 1) * LANES] = lines[
            pl.ds(line, cap, stride=LINES), :
        ]


def call(kernel, out_shapes, in_specs, scratch, cost, *args):
    single = not isinstance(out_shapes, list)
    return pl.pallas_call(
        kernel,
        out_shape=out_shapes,
        in_specs=in_specs,
        out_specs=VMEM if single else [VMEM] * len(out_shapes),
        scratch_shapes=scratch,
        compiler_params=pltpu.CompilerParams(vmem_limit_bytes=32 * 1024 * 1024),
        cost_estimate=pl.CostEstimate(flops=COST, bytes_accessed=COST, transcendentals=0),
    )(*args)


def shards(row_count, chip_count, hv, hp, hc, pv, pp, pc, sv, sp, sc, xp, xc):
    cap = hp.shape[1]
    rows = cap * LINES
    order = row_count * rows
    sends = rows // LANES
    f32 = jnp.float32

    def device(r, m, k):
        return (r * chip_count + m) * 2 + k

    def send(value, target):
        pairs = [
            (device(r, m, k), device(*target(r, m, k)))
            for r in range(row_count)
            for m in range(chip_count)
            for k in range(2)
            if target(r, m, k)
        ]
        return lax.ppermute(value, AXES, pairs)

    def to_other(value):
        return send(value, lambda r, m, k: (r, m, 1 - k))

    def stack(arrays, *others):
        return call(
            functools.partial(stack_kernel, len(others), len(arrays), rows),
            jax.ShapeDtypeStruct((len(arrays) * rows, LANES), f32),
            [pl.BlockSpec(memory_space=pl.ANY)] * len(others) + [VMEM] * len(arrays),
            [],
            1 << 10,
            *others, *arrays,
        )

    inputs = [
        pltpu.with_memory_space_constraint(x, pltpu.HBM) for x in (pp, pv, hv, sv, hp, sp, xp)
    ]

    def sized(extra):
        return jax.ShapeDtypeStruct((rows + extra, LANES), f32)

    tile, longer, longest = sized(0), sized(8), sized(16)
    lines = pltpu.VMEM((rows, LANES), f32)
    p_near, p_far, hv, sv, hp, sp, xp = call(
        first_kernel,
        [tile, longest] + [jax.ShapeDtypeStruct(x.shape, x.dtype) for x in inputs[2:]],
        [SMEM] + [pl.BlockSpec(memory_space=pltpu.HBM)] * 7,
        [
            pltpu.VMEM(pv.shape, f32),
            pltpu.VMEM(pp.shape, jnp.int32),
            lines,
            pltpu.SemaphoreType.DMA((7,)),
        ],
        1 << 10,
        pc, *inputs,
    )
    h_far, h_near, s_near, s_far, mask = call(
        rest_kernel,
        [tile, sized(32), sized(24), sized(40), jax.ShapeDtypeStruct((max(8, cap // 2), LANES), f32)],
        [VMEM] * 5 + [SMEM] * 3,
        [lines],
        1 << 10,
        hv, sv, hp, sp, xp, hc, sc, xc,
    )
    along = list(range(row_count - 1, 0, -1))
    across = list(range(chip_count - 1, 0, -1))

    def along_z(near, far, direct=False):
        got = {}

        def hops(offset):
            taken = []
            for bit in reversed(range(row_count.bit_length())):
                if offset >> bit & 1:
                    taken.append((2 << bit) - 1)
                    offset ^= taken[-1]
            return taken

        for offset in sorted(along, key=lambda s: len(hops(s))):
            hop = hops(offset)[-1]
            if offset != hop:
                value = got[offset ^ hop] if direct else stack([got[offset ^ hop]])
            else:
                value = near if hop == 1 else far
            got[offset] = send(value, lambda r, m, k: (r ^ hop, m, k))
        return [got[offset] for offset in along]

    def parted(x, count):
        return call(
            parted_kernel, [tile] * count, [VMEM], [], 1 << 10, x
        )

    def in_plane(x, other, others):
        return [
            send(other if o in others else x, lambda r, m, k, o=o: (r, m ^ o, k)) for o in across
        ]

    def product(a_got, a_shared, b, b_got, parts, *waits):
        part = jax.ShapeDtypeStruct((LANES, LANES), f32)
        return call(
            functools.partial(product_kernel, along, across, len(a_shared), len(waits)),
            [longer] + [part] * parts,
            [VMEM] * (3 + len(a_shared) + len(b_got))
            + [pl.BlockSpec(memory_space=pl.ANY)] * len(waits),
            [pltpu.VMEM((order, 2 * LANES), jnp.bfloat16)],
            1 << 10,
            a_got, *a_shared, b, *b_got, mask, *waits,
        )

    p_got = along_z(p_far, p_far)
    s_got = along_z(s_near, s_far)
    h_parts = [h_far] + in_plane(h_far, h_near, (1, 2))
    h_got = stack(h_parts, *p_got[::-1])
    h_shared = [to_other(x) for x in parted(h_got, len(h_parts))]
    (y,) = product(h_got, h_shared, p_near, p_got, 0)
    y_got = stack([y] + in_plane(y, y, ()), *s_got)
    x, *sent = product(y_got, [to_other(y_got)], s_near, s_got, sends)

    relay = row_count == chip_count == 4

    def mirror(turn):
        def target(r, m, k):
            column = 2 * m + k
            part = (column + turn) % sends
            if relay and turn == 0 and r ^ m < 2:
                return r, m ^ 1, part
            to = r * sends + part
            return column // sends, to // 2, to % 2

        return target

    mirrors = [send(value, mirror(turn)) for turn, value in enumerate(sent)]
    if relay:
        mirrors += [
            send(mirrors[0], lambda r, m, k: (r ^ 1, m, k) if r == m else None),
            sent[0],
            send(sent[1], lambda r, m, k: (r, m, 1 - k) if r == m else None),
        ]
    return call(
        functools.partial(slots_kernel, cap, sends),
        jax.ShapeDtypeStruct((1, cap, BS * BS), f32),
        [VMEM, SMEM] + [VMEM] * (1 + len(mirrors)),
        [lines] * 2,
        1 << 20,
        xp, xc, x, *mirrors,
    )


def solution(mesh):
    values, ints = P("row", "col", None), P("row", "col")
    row_count, col_count = mesh.shape["row"], mesh.shape["col"]
    return jax.shard_map(
        functools.partial(shards, row_count, col_count // 2),
        mesh=mesh,
        in_specs=(values, ints, ints) * 3 + (ints, ints),
        out_specs=values,
        check_vma=False,
    )
```
